128 devices in a mesh: space: 16 (over y, z), member: 8 (over x, core).
Axes of the slice: x: 4, y: 4, z: 4, core: 2. Of those that a mesh axis runs over, the one named last changes fastest.
Arguments:
- state_field: bfloat16 [8, 96, 1024, 256], P('member', None, 'space'), may hold values from -2.5 to 2.5
- context_field: bfloat16 [96, 1024, 256], P('member', 'space'), may hold values from -6 to 6
- noise_latent: bfloat16 [8, 1, 8, 1024, 256], P('member', None, None, 'space'), may hold values from -6 to 6
- gate_kernel: bfloat16 [192, 200, 3, 3], replicated, may hold values from -0.125 to 0.125
- candidate_kernel: bfloat16 [96, 200, 3, 3], replicated, may hold values from -0.125 to 0.125
- active_tiles: int32 [16, 4], replicated, may hold values from 0 to 1, as said below
- tile_offset: int32 [16, 4], replicated, may hold values from 0 to 3, as said below
Outputs:
- next_state: bfloat16 [8, 96, 1024, 256], P('member', None, 'space')
The draws below stay inside these ranges and needn't reach their ends.
Inputs may be any that keep to these rules, and one draw needn't show every extreme that they name: `active_tiles`: each owner has between 1 and 3 active tiles, and some owner has exactly 3; its tile with tile_offset 0 is always active. Each row is a permutation of 0 .. 3; active tiles have tile_offset below 3. An active tile of owner s with tile_offset k is computed by owner (s + k) mod 16; each owner computes at most 2 tiles counting its own, and some owner computes exactly 2.
All inputs are finite; a program needn't handle non-finite values.
Results may differ from the reference program's by a relative error of at most 0.001.
Values may be sent and summed in bfloat16 or wider, within the bound.
No kernel may reach another device: no remote copies, remote signals or barrier semaphores. Data moves between devices by JAX's collectives and lax.ppermute only.
A program may use at most 128 MiB of HBM per device.

```python
import jax
import jax.numpy as jnp
from jax import lax

STATE_CH = 96
CONTEXT_CH = 96
NOISE_CH = 8
TILE = 64
STEPS = 1
TILES_ROW = 4
REACH = 3
WORK = 2
HALO = 2
OWNERS = 16
MEMBERS = 8
ROWS = 1024
COLS = 256


def tile_plan(key):
    keys = jax.random.split(key, 4)
    extra = jax.random.randint(keys[0], (OWNERS,), 1, REACH)
    extra = extra.at[0].set(1).at[2].set(2)
    storm = jax.random.randint(keys[2], (), 3, OWNERS - REACH + 1)
    receivers = jnp.arange(OWNERS)
    relative = (receivers - storm) % OWNERS
    forced = (relative >= 1) & (relative <= REACH - 1)
    extra = jnp.where(forced, relative, extra)
    offsets = jnp.arange(REACH)
    target = (receivers[:, None] + offsets[None, :]) % OWNERS
    sent = (offsets[None, :] == 0) | (extra[target] == offsets[None, :])

    def shuffle(row_key):
        return jax.random.permutation(row_key, TILES_ROW)
    perms = jax.vmap(shuffle)(jax.random.split(keys[3], OWNERS))
    ranks = jnp.broadcast_to(jnp.arange(TILES_ROW), (OWNERS, TILES_ROW))
    placing = jnp.zeros((OWNERS, TILES_ROW), jnp.int32).at[receivers[:, None], perms].set(ranks)
    lookup = jnp.minimum(placing, REACH - 1)
    active = ((placing < REACH) & jnp.take_along_axis(sent, lookup, axis=1)).astype(jnp.int32)
    return (active, placing.astype(jnp.int32))


def draw_active_tiles(key, part):
    active, placing = tile_plan(key)
    return active


def draw_tile_offset(key, part):
    active, placing = tile_plan(key)
    return placing


def levels(rng, shape, pieces, smallest, top_value):
    factor_of = 1.0
    for position, blocks in pieces:
        draws = jax.random.uniform(jax.random.fold_in(jax.random.fold_in(rng, 6), position), (blocks,), jnp.float32, smallest / len(pieces), top_value / len(pieces))
        factor_of = factor_of * jnp.repeat(jnp.exp(draws), shape[position] // blocks).reshape((-1,) + (1,) * (len(shape) - 1 - position))
    return factor_of


def noise(stream_key, shape, scale, reach, cuts=(), kind=jnp.bfloat16):
    factor_of = levels(stream_key, shape, cuts, -0.22, 0.18) if cuts else 1.0
    values = jax.random.normal(stream_key, shape, jnp.float32) * scale * factor_of
    return jnp.minimum(jnp.maximum(values, -reach), reach).astype(kind)


def setup_inputs(seed: int = 0) -> dict:
    splits = jax.random.split(jax.random.key(seed), 8)
    state_field = noise(splits[0], (MEMBERS, STATE_CH, ROWS, COLS), 0.6, 2.5, ((0, 8), (2, 16)))
    context_field = noise(splits[1], (CONTEXT_CH, ROWS, COLS), 1.0, 6.0, ((0, 8), (1, 16)))
    noise_latent = noise(splits[2], (MEMBERS, STEPS, NOISE_CH, ROWS, COLS), 1.0, 6.0, ((0, 8), (3, 16)))
    gate_kernel = noise(splits[3], (2 * STATE_CH, STATE_CH + CONTEXT_CH + NOISE_CH, 3, 3), (9 * (STATE_CH + CONTEXT_CH + NOISE_CH)) ** -0.5, 0.125)
    candidate_kernel = noise(splits[4], (STATE_CH, STATE_CH + CONTEXT_CH + NOISE_CH, 3, 3), (9 * (STATE_CH + CONTEXT_CH + NOISE_CH)) ** -0.5, 0.125)
    active_tiles = draw_active_tiles(jax.random.fold_in(splits[7], 71), 0)
    tile_offset = draw_tile_offset(jax.random.fold_in(splits[7], 71), 0)
    return {"state_field": state_field, "context_field": context_field, "noise_latent": noise_latent, "gate_kernel": gate_kernel, "candidate_kernel": candidate_kernel, "active_tiles": active_tiles, "tile_offset": tile_offset}


def convolve(inputs, kernel):
    return lax.conv_general_dilated(inputs.astype(jnp.float32), kernel.astype(jnp.float32), (1, 1), "VALID", dimension_numbers=("NCHW", "OIHW", "NCHW"), precision=lax.Precision.HIGHEST)


def trimmed(values, margin):
    return values[:, :, margin:values.shape[2] - margin, margin:values.shape[3] - margin]


def recurrent_step(carried, context, noise_part, gate_kernel, candidate_kernel):
    joined = jnp.concatenate([carried, context, noise_part], axis=1)
    gate_terms = convolve(joined, gate_kernel)
    update = jax.nn.sigmoid(gate_terms[:, :STATE_CH])
    reset_gate = jax.nn.sigmoid(gate_terms[:, STATE_CH:])
    reset_state = (reset_gate * trimmed(carried, 1).astype(jnp.float32)).astype(jnp.bfloat16)
    joined = jnp.concatenate([reset_state, trimmed(context, 1), trimmed(noise_part, 1)], axis=1)
    proposal = jnp.tanh(convolve(joined, candidate_kernel))
    update = trimmed(update, 1)
    return (1.0 - update) * trimmed(carried, 2).astype(jnp.float32) + update * proposal


def advance(window, gate_kernel, candidate_kernel):
    carried = window[:, :STATE_CH]
    context = window[:, STATE_CH:STATE_CH + CONTEXT_CH]
    noises = window[:, STATE_CH + CONTEXT_CH:]
    for lead_step in range(STEPS):
        margin = 2 * lead_step
        noise_part = noises[:, lead_step * NOISE_CH:(lead_step + 1) * NOISE_CH]
        carried = recurrent_step(carried, trimmed(context, margin), trimmed(noise_part, margin), gate_kernel, candidate_kernel).astype(jnp.bfloat16)
    return carried


def reference(state_field, context_field, noise_latent, gate_kernel, candidate_kernel, active_tiles, tile_offset):
    members = state_field.shape[0]
    extent = TILE + 2 * HALO
    padding = ((0, 0), (0, 0), (HALO, HALO), (HALO, HALO))
    padded_state = jnp.pad(state_field, padding)
    padded_context = jnp.pad(context_field[None], padding)
    padded_noise = jnp.pad(noise_latent.reshape(members, STEPS * NOISE_CH, ROWS, COLS), padding)
    offsets = jnp.arange(REACH, dtype=jnp.int32)
    selected = (active_tiles[:, None, :] == 1) & (tile_offset[:, None, :] == offsets[None, :, None])
    in_use = jnp.any(selected, axis=2)
    tile_index = jnp.arange(TILES_ROW, dtype=jnp.int32)
    columns = jnp.sum(jnp.where(selected, tile_index[None, None, :], 0), axis=2).astype(jnp.int32).reshape(-1)
    job_order = jnp.nonzero(in_use.reshape(-1), size=WORK * OWNERS, fill_value=0)[0].astype(jnp.int32)
    job_count = jnp.sum(in_use.astype(jnp.int32))
    zero = jnp.int32(0)

    def run_job(job, updated):
        pair_index = job_order[job]
        row_start = (pair_index // REACH).astype(jnp.int32) * TILE
        col_start = columns[pair_index] * TILE
        start = (zero, zero, row_start, col_start)
        window = jnp.concatenate([
            lax.dynamic_slice(padded_state, start, (members, STATE_CH, extent, extent)),
            jnp.broadcast_to(lax.dynamic_slice(padded_context, start, (1, CONTEXT_CH, extent, extent)), (members, CONTEXT_CH, extent, extent)),
            lax.dynamic_slice(padded_noise, start, (members, STEPS * NOISE_CH, extent, extent))], axis=1)
        result = advance(window, gate_kernel, candidate_kernel)
        current = lax.dynamic_slice(updated, start, (members, STATE_CH, TILE, TILE))
        return lax.dynamic_update_slice(updated, jnp.where(job < job_count, result, current), start)

    return lax.fori_loop(0, WORK * OWNERS, run_job, state_field)
```

```python
import functools

import jax
import jax.numpy as jnp
from jax import lax
from jax.experimental import pallas as pl
from jax.experimental.pallas import tpu as pltpu
from jax.sharding import PartitionSpec as P

STATE_CH = 96
CONTEXT_CH = 96
NOISE_CH = 8
TILE = 64
REACH = 3
HALO = 2
ROWS = 64
COLS = 256
CHUNK = 16
STEPS = ROWS // CHUNK
SIDE_CH = CONTEXT_CH + 16
PIECE = CONTEXT_CH // 8
S3 = 3 * STATE_CH
C3 = 3 * SIDE_CH
BF16 = jnp.bfloat16
F32 = jnp.float32


def put_taps(ref, first, row):
    count = row.shape[0]
    edge = jnp.zeros((count, 1), row.dtype)
    ref[pl.ds(first, count), :] = jnp.concatenate([edge, row[:, : COLS - 1]], axis=1)
    ref[pl.ds(first + count, count), :] = row
    ref[pl.ds(first + 2 * count, count), :] = jnp.concatenate([row[:, 1:], edge], axis=1)


def logistic(x):
    return 0.5 * jnp.tanh(0.5 * x) + 0.5


def state_kernel(state, rim, weights, sums, first_sums, by_row, taps):
    step = pl.program_id(0)

    def sums_at(place):
        start = pl.multiple_of(place * S3, 16)
        return jnp.dot(weights[...], taps[pl.ds(start, 3 * S3), :], preferred_element_type=F32)

    @pl.when(step == 0)
    def _():
        chunk = jnp.transpose(state[:, :CHUNK, :], (1, 0, 2))
        for n in range(HALO):
            put_taps(taps, n * S3, rim[n])
            put_taps(taps, (HALO + ROWS + n) * S3, rim[HALO + n])
        for n in range(CHUNK):
            put_taps(taps, (HALO + n) * S3, chunk[n])
        for n in range(HALO):
            first_sums[n] = sums_at(n)

    here = pl.multiple_of(step * CHUNK, CHUNK)
    by_row[...] = jnp.transpose(state[:, pl.ds(here, CHUNK), :], (1, 0, 2))
    later = jnp.minimum(step + 1, STEPS - 1) * CHUNK
    chunk = jnp.transpose(state[:, pl.ds(pl.multiple_of(later, CHUNK), CHUNK), :], (1, 0, 2))
    for n in range(CHUNK):
        put_taps(taps, pl.multiple_of((HALO + later + n) * S3, 16), chunk[n])
        if n >= HALO:
            sums[n - HALO] = sums_at(here + n)
    for n in range(CHUNK - HALO, CHUNK):
        sums[n] = sums_at(here + n + HALO)


def side_kernel(
    pieces, noise, side_rim, by_row, rim, sums, first_sums, side_weights, reset_weights, active, offset,
    out, raw, taps, reset_taps, update, partial, rows_done, sems,
):
    step = pl.program_id(0)
    here = pl.multiple_of(step * CHUNK, CHUNK)

    def sums_at(place):
        start = pl.multiple_of(place * C3, 16)
        return jnp.dot(side_weights[...], taps[pl.ds(start, 3 * C3), :], preferred_element_type=F32)

    def gates(row_sums, state_sums, carried, slot):
        update[slot] = logistic(row_sums[:STATE_CH] + state_sums[:STATE_CH])
        reset = logistic(row_sums[STATE_CH : 2 * STATE_CH] + state_sums[STATE_CH:])
        partial[slot] = row_sums[2 * STATE_CH :]
        put_taps(reset_taps, slot * S3, (reset * carried.astype(F32)).astype(BF16))

    @pl.when(step == 0)
    def _():
        member = lax.axis_index("member")
        x, core = member // 2, member % 2
        copies = []
        for n, piece in enumerate(pieces):
            shift, rows, other = ((0, 0, ROWS), (3, 0, ROWS), (1, 0, ROWS), (2, 0, ROWS // 2), (2, ROWS // 2, ROWS // 2))[n % 5], None, n // 5
            place = 2 * lax.rem(x + shift[0], 4) + (core if other == 0 else 1 - core)
            target = raw.at[pl.ds(place * PIECE, PIECE), pl.ds(shift[1], shift[2]), :]
            copies.append(pltpu.make_async_copy(piece, target, sems.at[n]))
        for copy in copies:
            copy.start()
        raw[CONTEXT_CH : CONTEXT_CH + NOISE_CH] = noise[...]
        raw[CONTEXT_CH + NOISE_CH :] = jnp.zeros((SIDE_CH - CONTEXT_CH - NOISE_CH, ROWS, COLS), BF16)
        for n in range(HALO):
            put_taps(taps, n * C3, side_rim[n])
            put_taps(taps, (HALO + ROWS + n) * C3, side_rim[HALO + n])
        for copy in copies:
            copy.wait()
        chunk = jnp.transpose(raw[:, :CHUNK, :], (1, 0, 2))
        for n in range(CHUNK):
            put_taps(taps, (HALO + n) * C3, chunk[n])
        gates(sums_at(0), first_sums[0], rim[HALO - 1], 0)
        gates(sums_at(1), first_sums[1], by_row[0], 1)

    @pl.when(step > 0)
    def _():
        reset_taps[: 2 * S3] = reset_taps[CHUNK * S3 :]
        update[1] = update[CHUNK + 1]
        partial[1] = partial[CHUNK + 1]

    later = jnp.minimum(step + 1, STEPS - 1) * CHUNK
    chunk = jnp.transpose(raw[:, pl.ds(pl.multiple_of(later, CHUNK), CHUNK), :], (1, 0, 2))

    def gate_row(n):
        row = here + n + 1
        carried = by_row[jnp.minimum(row, ROWS - 1)]
        if n == CHUNK - 1:
            carried = jnp.where(step == STEPS - 1, rim[HALO], carried)
        gates(sums_at(here + n + 2), sums[n], carried, n + 2)

    for n in range(CHUNK):
        put_taps(taps, pl.multiple_of((HALO + later + n) * C3, 16), chunk[n])
        if n >= HALO:
            gate_row(n - HALO)
    for n in range(CHUNK - HALO, CHUNK):
        gate_row(n)

    owner = lax.axis_index("space")
    tile = lax.broadcasted_iota(jnp.int32, (1, COLS), 1) // TILE
    chosen = jnp.zeros((1, COLS), jnp.bool_)
    for n in range(COLS // TILE):
        used = (active[owner, n] == 1) & (offset[owner, n] < REACH)
        chosen = chosen | ((tile == n) & used)
    for n in range(CHUNK):
        terms = jnp.dot(reset_weights[...], reset_taps[n * S3 : (n + 3) * S3, :], preferred_element_type=F32)
        proposal = jnp.tanh(terms + partial[n + 1])
        old = by_row[here + n].astype(F32)
        new = (1.0 - update[n + 1]) * old + update[n + 1] * proposal
        rows_done[n] = jnp.where(chosen, new, old).astype(BF16)
    out[...] = jnp.transpose(rows_done[...], (1, 0, 2))


def whole(*shape):
    return pl.BlockSpec(shape, lambda i: (0,) * len(shape))


def state_part(state, rim, weights):
    return pl.pallas_call(
        state_kernel,
        grid=(STEPS,),
        in_specs=[whole(STATE_CH, ROWS, COLS), whole(2 * HALO, STATE_CH, COLS), whole(2 * STATE_CH, 3 * S3)],
        out_specs=[
            pl.BlockSpec((CHUNK, 2 * STATE_CH, COLS), lambda i: (i, 0, 0)),
            whole(HALO, 2 * STATE_CH, COLS),
            pl.BlockSpec((CHUNK, STATE_CH, COLS), lambda i: (i, 0, 0)),
        ],
        out_shape=[
            jax.ShapeDtypeStruct((ROWS, 2 * STATE_CH, COLS), F32),
            jax.ShapeDtypeStruct((HALO, 2 * STATE_CH, COLS), F32),
            jax.ShapeDtypeStruct((ROWS, STATE_CH, COLS), BF16),
        ],
        scratch_shapes=[pltpu.VMEM(((ROWS + 2 * HALO) * S3, COLS), BF16)],
        compiler_params=pltpu.CompilerParams(vmem_limit_bytes=50 * 2**20),
        cost_estimate=pl.CostEstimate(flops=11_000_000_000, bytes_accessed=20_000_000, transcendentals=0),
        name="state_part",
    )(state, rim, weights)


def side_part(pieces, noise, side_rim, by_row, rim, sums, first_sums, side_weights, reset_weights, active, offset):
    count = len(pieces)

    def kernel(*refs):
        side_kernel(refs[:count], *refs[count:])

    smem = pl.BlockSpec(memory_space=pltpu.SMEM)
    return pl.pallas_call(
        kernel,
        grid=(STEPS,),
        in_specs=[pl.BlockSpec(memory_space=pl.ANY)] * count
        + [
            whole(NOISE_CH, ROWS, COLS),
            whole(2 * HALO, SIDE_CH, COLS),
            whole(ROWS, STATE_CH, COLS),
            whole(2 * HALO, STATE_CH, COLS),
            pl.BlockSpec((CHUNK, 2 * STATE_CH, COLS), lambda i: (i, 0, 0)),
            whole(HALO, 2 * STATE_CH, COLS),
            whole(3 * STATE_CH, 3 * C3),
            whole(STATE_CH, 3 * S3),
            smem,
            smem,
        ],
        out_specs=pl.BlockSpec((STATE_CH, CHUNK, COLS), lambda i: (0, i, 0)),
        out_shape=jax.ShapeDtypeStruct((STATE_CH, ROWS, COLS), BF16),
        scratch_shapes=[
            pltpu.VMEM((SIDE_CH, ROWS, COLS), BF16),
            pltpu.VMEM(((ROWS + 2 * HALO) * C3, COLS), BF16),
            pltpu.VMEM(((CHUNK + 2) * S3, COLS), BF16),
            pltpu.VMEM((CHUNK + 2, STATE_CH, COLS), F32),
            pltpu.VMEM((CHUNK + 2, STATE_CH, COLS), F32),
            pltpu.VMEM((CHUNK, STATE_CH, COLS), BF16),
            pltpu.SemaphoreType.DMA((count,)),
        ],
        compiler_params=pltpu.CompilerParams(vmem_limit_bytes=56 * 2**20),
        cost_estimate=pl.CostEstimate(flops=17_000_000_000, bytes_accessed=20_000_000, transcendentals=0),
        name="side_part",
    )(*pieces, noise, side_rim, by_row, rim, sums, first_sums, side_weights, reset_weights, active, offset)


def tap_weights(kernel, first, count, padded):
    taps = jnp.transpose(kernel[:, first : first + count], (2, 3, 0, 1))
    taps = jnp.pad(taps, ((0, 0), (0, 0), (0, 0), (0, padded - count)))
    return jnp.concatenate([taps[a, b] for a in range(3) for b in range(3)], axis=1)


def along_x(by):
    return [(2 * x + core, 2 * ((x + by) % 4) + core) for x in range(4) for core in range(2)]


CORES = [(n, n ^ 1) for n in range(8)]


def gathered_pieces(context):
    half = ROWS // 2
    right = lax.ppermute(context, "member", along_x(1))
    left = lax.ppermute(context, "member", along_x(-1))
    right_far = lax.ppermute(right[:, :half], "member", along_x(1))
    left_far = lax.ppermute(left[:, half:], "member", along_x(-1))
    mine = [context, right, left, right_far, left_far]
    return mine + [lax.ppermute(piece, "member", CORES) for piece in mine]


def gathered_rim(rim):
    member = lax.axis_index("member")
    far = [lax.ppermute(rim, "member", along_x(by)) for by in (3, 2, 1)]
    mine = jnp.stack([rim] + far)
    other = lax.ppermute(mine, "member", CORES)
    x, core = member // 2, member % 2
    pair = jnp.where(core == 0, jnp.stack([mine, other], axis=1), jnp.stack([other, mine], axis=1))
    pair = jnp.concatenate([pair, pair], axis=0)
    pair = lax.dynamic_slice_in_dim(pair, lax.rem(4 - x, 4), 4, axis=0)
    return jnp.transpose(pair, (2, 0, 1, 3, 4)).reshape(2 * HALO, CONTEXT_CH, COLS)


def shards(state_field, context_field, noise_latent, gate_kernel, candidate_kernel, active_tiles, tile_offset):
    owners = lax.axis_size("space")
    state = state_field[0]
    noise = noise_latent[0, 0]
    pieces = gathered_pieces(context_field)

    def edge(first):
        rows = [a[:, first : first + HALO] for a in (state, context_field, noise)]
        return jnp.transpose(jnp.concatenate(rows, axis=0), (1, 0, 2))

    down = [(n, n + 1) for n in range(owners - 1)]
    up = [(n + 1, n) for n in range(owners - 1)]
    above = lax.ppermute(edge(ROWS - HALO), "space", down)
    below = lax.ppermute(edge(0), "space", up)
    rims = jnp.concatenate([above, below], axis=0)
    rim = rims[:, :STATE_CH]
    state_weights = tap_weights(gate_kernel, 0, STATE_CH, STATE_CH)
    sums, first_sums, by_row = state_part(state, rim, state_weights)
    side_kernels = jnp.concatenate([gate_kernel[:, STATE_CH:], candidate_kernel[:, STATE_CH:]], axis=0)
    side_weights = tap_weights(side_kernels, 0, CONTEXT_CH + NOISE_CH, SIDE_CH)
    reset_weights = tap_weights(candidate_kernel, 0, STATE_CH, STATE_CH)
    side_rim = jnp.concatenate(
        [
            gathered_rim(rims[:, STATE_CH : STATE_CH + PIECE]),
            rims[:, STATE_CH + PIECE :],
            jnp.zeros((2 * HALO, SIDE_CH - CONTEXT_CH - NOISE_CH, COLS), BF16),
        ],
        axis=1,
    )
    result = side_part(
        pieces, noise, side_rim, by_row, rim, sums, first_sums, side_weights, reset_weights, active_tiles, tile_offset
    )
    return result[None]


def solution(mesh):
    return jax.shard_map(
        shards,
        mesh=mesh,
        in_specs=(
            P("member", None, "space", None),
            P("member", "space", None),
            P("member", None, None, "space", None),
            P(),
            P(),
            P(),
            P(),
        ),
        out_specs=P("member", None, "space", None),
        check_vma=False,
    )
```

```python
import functools

import jax
import jax.numpy as jnp
from jax import lax
from jax.experimental import pallas as pl
from jax.experimental.pallas import tpu as pltpu
from jax.sharding import PartitionSpec as P

STATE_CH = 96
CONTEXT_CH = 96
NOISE_CH = 8
TILE = 64
REACH = 3
HALO = 2
ROWS = 64
COLS = 256
CHUNK = 16
STEPS = ROWS // CHUNK
SIDE_CH = CONTEXT_CH + 16
PIECE = CONTEXT_CH // 8
EDGE_CH = STATE_CH + 32
S3 = 3 * STATE_CH
C3 = 3 * SIDE_CH
BF16 = jnp.bfloat16
F32 = jnp.float32


def put_taps(ref, first, row):
    count = row.shape[0]
    edge = jnp.zeros((count, 1), row.dtype)
    ref[pl.ds(first, count), :] = jnp.concatenate([edge, row[:, : COLS - 1]], axis=1)
    ref[pl.ds(first + count, count), :] = row
    ref[pl.ds(first + 2 * count, count), :] = jnp.concatenate([row[:, 1:], edge], axis=1)


def logistic(x):
    return 0.5 * jnp.tanh(0.5 * x) + 0.5


def edge_kernel(state_top, state_low, noise_top, noise_low, context_top, context_low, top, low):
    def fill(ref, first, state, noise, context):
        def rows(a):
            return jnp.transpose(a[...], (1, 0, 2))[first : first + HALO]

        ref[:, :STATE_CH] = rows(state)
        ref[:, STATE_CH:] = jnp.zeros((HALO, EDGE_CH - STATE_CH, COLS), BF16)
        ref[:, STATE_CH : STATE_CH + NOISE_CH] = rows(noise)
        ref[:, STATE_CH + 16 : STATE_CH + 16 + PIECE] = rows(context)

    fill(top, 0, state_top, noise_top, context_top)
    fill(low, CHUNK - HALO, state_low, noise_low, context_low)


def edges(state, noise, context):
    def block(channels, n):
        return pl.BlockSpec((channels, CHUNK, COLS), lambda i: (0, n, 0))

    last = ROWS // CHUNK - 1
    shape = jax.ShapeDtypeStruct((HALO, EDGE_CH, COLS), BF16)
    return pl.pallas_call(
        edge_kernel,
        grid=(1,),
        in_specs=[block(count, n) for count in (STATE_CH, NOISE_CH, PIECE) for n in (0, last)],
        out_specs=[whole(HALO, EDGE_CH, COLS)] * 2,
        out_shape=[shape, shape],
        compiler_params=pltpu.CompilerParams(vmem_limit_bytes=60 * 2**20),
        cost_estimate=pl.CostEstimate(flops=0, bytes_accessed=4_000_000, transcendentals=0),
        name="edges",
    )(state, state, noise, noise, context, context)


def joined_taps(kernel, first, count, padded):
    parts = []
    for tap in range(9):
        parts.append(kernel[tap, :, first : first + count])
        if padded > count:
            parts.append(jnp.zeros((kernel.shape[1], padded - count), BF16))
    return jnp.concatenate(parts, axis=1)


def inside(row, is_inside):
    return jnp.where(is_inside, row, jnp.zeros_like(row))


def state_kernel(first, count, *refs):
    state, following, kernel = refs[:3]
    last = first + count == STEPS
    if last:
        above, below, top = refs[3:6]
        sums, by_row, rim_sums, taps, weights, sums_buf, sems, rim_taps = refs[8:]
    else:
        sums, by_row, taps, weights, sums_buf, sems = refs[3:]
    turn = pl.program_id(0)
    half = CHUNK // 2

    def sums_copy(part, n):
        start = pl.multiple_of((first + part) * CHUNK + n * half, half)
        source = sums_buf.at[part, pl.ds(n * half, half)]
        return pltpu.make_async_copy(source, sums.at[pl.ds(start, half)], sems.at[part, n])

    def sums_at(ref, place):
        return jnp.dot(weights[...], ref[place * S3 : (place + 3) * S3, :], preferred_element_type=F32)

    here = jnp.transpose(state[...], (1, 0, 2))
    by_row[...] = here

    @pl.when(turn == 0)
    def _():
        weights[...] = joined_taps(kernel, 0, STATE_CH, STATE_CH)
        for n in range(CHUNK):
            put_taps(taps, n * S3, here[n])
        if last:
            not_first = lax.axis_index("space") > 0
            for n in range(HALO):
                put_taps(rim_taps, n * S3, inside(above[n, :STATE_CH], not_first))
                put_taps(rim_taps, (HALO + n) * S3, top[n, :STATE_CH])
            for n in range(HALO):
                rim_sums[n] = sums_at(rim_taps, n)

    rows = jnp.transpose(following[...], (1, 0, 2))
    for n in range(CHUNK):
        sums_buf[turn, n] = sums_at(taps, n)
        if n == half - 1:
            sums_copy(turn, 0).start()
        row = rows[n]
        if n < HALO:
            if last:
                not_last = lax.axis_index("space") < lax.axis_size("space") - 1
                row = jnp.where(turn == count - 1, inside(below[n, :STATE_CH], not_last), row)
            put_taps(taps, (CHUNK + n) * S3, row)
        put_taps(taps, n * S3, row)
    sums_copy(turn, 1).start()

    @pl.when(turn == count - 1)
    def _():
        for part in range(count):
            for n in range(2):
                sums_copy(part, n).wait()


def state_part(first, count, state, kernel, rims=None, before=None):
    last = first + count == STEPS
    extra = [*rims, *before] if last else []
    any_space = pl.BlockSpec(memory_space=pl.ANY)
    shapes = [
        jax.ShapeDtypeStruct((ROWS, 2 * STATE_CH, COLS), F32),
        jax.ShapeDtypeStruct((ROWS, STATE_CH, COLS), BF16),
    ]
    specs = [any_space, pl.BlockSpec((CHUNK, STATE_CH, COLS), lambda i: (first + i, 0, 0))]
    scratch = [
        pltpu.VMEM(((CHUNK + HALO) * S3, COLS), BF16),
        pltpu.VMEM((2 * STATE_CH, 3 * S3), BF16),
        pltpu.VMEM((count, CHUNK, 2 * STATE_CH, COLS), F32),
        pltpu.SemaphoreType.DMA((count, 2)),
    ]
    if last:
        shapes.append(jax.ShapeDtypeStruct((HALO, 2 * STATE_CH, COLS), F32))
        specs.append(whole(HALO, 2 * STATE_CH, COLS))
        scratch.append(pltpu.VMEM((2 * HALO * S3, COLS), BF16))
    return pl.pallas_call(
        functools.partial(state_kernel, first, count),
        grid=(count,),
        in_specs=[
            pl.BlockSpec((STATE_CH, CHUNK, COLS), lambda i: (0, first + i, 0)),
            pl.BlockSpec((STATE_CH, CHUNK, COLS), lambda i: (0, jnp.minimum(first + i + 1, STEPS - 1), 0)),
            whole(*kernel.shape),
        ]
        + ([whole(HALO, EDGE_CH, COLS)] * 3 + [any_space] * 2 if last else []),
        out_specs=specs,
        out_shape=shapes,
        scratch_shapes=scratch,
        input_output_aliases={6: 0, 7: 1} if last else {},
        compiler_params=pltpu.CompilerParams(vmem_limit_bytes=60 * 2**20),
        cost_estimate=pl.CostEstimate(flops=3_000_000_000 * count, bytes_accessed=5_000_000 * count, transcendentals=0),
        name="state_part_%d" % first,
    )(state, state, kernel, *extra)


LAG = 3
MAIN = 256
REST = S3 - MAIN


def side_kernel(
    mine, others, noise, mine_rim, other_rim, above, below, sums, by_row, rim_sums, gate_kernel, candidate_kernel,
    active, offset, out, raw, w_side, w_reset, w_rest, sums_buf, rows_buf, rim_sums_buf, taps, rim_taps, reset_taps,
    rest_taps, update, partial, rows_done, context_rim, gate_buf, candidate_buf, piece_sems, sums_sems, sems,
):
    step = pl.program_id(0)
    half = ROWS // 2
    member = lax.axis_index("member")
    x, core = member // 2, member % 2

    def piece_copies(part):
        copies = []
        for n in range(8):
            piece = (mine if n < 4 else others)[n % 4]
            side = core if n < 4 else 1 - core
            near = 3 - 2 * side
            place = 2 * lax.rem(x + (0, near, 4 - near, 2)[n % 4], 4) + side
            rows = pl.ds(part * half, half)
            target = raw.at[pl.ds(place * PIECE, PIECE), rows, :]
            copies.append(pltpu.make_async_copy(piece.at[:, rows, :], target, piece_sems.at[part, n]))
        copies.append(
            pltpu.make_async_copy(
                noise.at[:, pl.ds(part * half, half), :],
                raw.at[pl.ds(CONTEXT_CH, NOISE_CH), pl.ds(part * half, half), :],
                piece_sems.at[part, 8],
            )
        )
        return copies

    def sums_copy(n):
        slot = lax.rem(n, 2)
        rows = pl.ds(pl.multiple_of(n * CHUNK, CHUNK), CHUNK)
        return pltpu.make_async_copy(sums.at[rows], sums_buf.at[slot], sums_sems.at[slot])

    def sums_at(ref, place):
        return jnp.dot(w_side[...], ref[place * C3 : (place + 3) * C3, :], preferred_element_type=F32)

    not_first = lax.axis_index("space") > 0
    not_last = lax.axis_index("space") < lax.axis_size("space") - 1

    def gates(row_sums, state_sums, carried, slots):
        reset = logistic(row_sums[STATE_CH : 2 * STATE_CH] + state_sums[STATE_CH:])
        reset_row = (reset * carried.astype(F32)).astype(BF16)
        kept = logistic(row_sums[:STATE_CH] + state_sums[:STATE_CH])
        edge = jnp.zeros((STATE_CH, 1), BF16)
        right = jnp.concatenate([reset_row[:, 1:], edge], axis=1)
        first = slots[0] % 4 * MAIN
        reset_taps[first : first + STATE_CH] = jnp.concatenate([edge, reset_row[:, : COLS - 1]], axis=1)
        reset_taps[first + STATE_CH : first + 2 * STATE_CH] = reset_row
        reset_taps[first + 2 * STATE_CH : first + MAIN] = right[: MAIN - 2 * STATE_CH]
        for slot in slots:
            rest_taps[slot * REST : (slot + 1) * REST] = right[MAIN - 2 * STATE_CH :]
            update[slot] = kept

    def candidate_terms(slot, side_terms):
        first = slot % 4 * MAIN
        terms = jnp.dot(w_reset[...], reset_taps[first : first + MAIN, :], preferred_element_type=F32)
        partial[slot + 1] = terms[:STATE_CH]
        if slot > 0:
            partial[slot] += terms[STATE_CH : 2 * STATE_CH] + side_terms
        return terms[2 * STATE_CH :]

    @pl.when(step == 0)
    def _():
        raw[CONTEXT_CH + NOISE_CH :] = jnp.zeros((SIDE_CH - CONTEXT_CH - NOISE_CH, ROWS, COLS), BF16)
        first_half = piece_copies(0)
        for copy in first_half:
            copy.start()
        rest = [
            pltpu.make_async_copy(a, b, sems.at[n])
            for n, (a, b) in enumerate(
                ((gate_kernel, gate_buf), (candidate_kernel, candidate_buf), (rim_sums, rim_sums_buf), (by_row, rows_buf))
            )
        ]
        for copy in rest:
            copy.start()
        sums_copy(0).start()
        for copy in piece_copies(1):
            copy.start()
        for copy in rest[:2]:
            copy.wait()
        channels = CONTEXT_CH + NOISE_CH
        w_side[: 2 * STATE_CH] = joined_taps(gate_buf, STATE_CH, channels, SIDE_CH)
        w_side[2 * STATE_CH :] = joined_taps(candidate_buf, STATE_CH, channels, SIDE_CH)
        for a in range(3):
            left, middle, right = (candidate_buf[3 * a + n, :, :STATE_CH] for n in range(3))
            w_reset[a * STATE_CH : (a + 1) * STATE_CH] = jnp.concatenate(
                [left, middle, right[:, : MAIN - 2 * STATE_CH]], axis=1
            )
        w_rest[...] = jnp.concatenate(
            [candidate_buf[3 * a + 2, :, MAIN - 2 * STATE_CH : STATE_CH] for a in range(3)], axis=1
        )
        for n in range(2 * HALO):
            parts = []
            for place in range(4):
                turned = lax.rem(place + 4 - x, 4)
                a, b = mine_rim[turned, n].astype(F32), other_rim[turned, n].astype(F32)
                parts += [jnp.where(core == 0, a, b), jnp.where(core == 0, b, a)]
            context_rim[n] = inside(jnp.concatenate(parts, axis=0), not_first if n < HALO else not_last).astype(BF16)
        for copy in first_half:
            copy.wait()
        chunk = jnp.transpose(raw[:, :CHUNK, :], (1, 0, 2))
        for n in range(HALO):
            noise_rim = inside(above[n, STATE_CH : STATE_CH + 16], not_first)
            put_taps(rim_taps, n * C3, jnp.concatenate([context_rim[n], noise_rim], axis=0))
            put_taps(rim_taps, (HALO + n) * C3, chunk[n])
        for n in range(CHUNK):
            put_taps(taps, n * C3, chunk[n])
        for copy in rest[2:]:
            copy.wait()
        gates(sums_at(rim_taps, 0), rim_sums_buf[0], inside(above[1, :STATE_CH], not_first), (0,))
        candidate_terms(0, None)
        row_sums = sums_at(rim_taps, 1)
        gates(row_sums, rim_sums_buf[1], rows_buf[0], (1,))
        candidate_terms(1, row_sums[2 * STATE_CH :])

    @pl.when(step == 1)
    def _():
        for copy in piece_copies(1):
            copy.wait()

    @pl.when(step + 1 < STEPS)
    def _():
        sums_copy(step + 1).start()

    sums_copy(step).wait()
    state_sums = sums_buf.at[lax.rem(step, 2)]
    here = pl.multiple_of(step * CHUNK, CHUNK)
    owner = lax.axis_index("space")
    tile = lax.broadcasted_iota(jnp.int32, (1, COLS), 1) // TILE
    chosen = jnp.zeros((1, COLS), jnp.bool_)
    for n in range(COLS // TILE):
        used = (active[n, owner] == 1) & (offset[n, owner] < REACH)
        chosen = chosen | ((tile == n) & used)
    later = jnp.minimum(step + 1, STEPS - 1) * CHUNK
    chunk = jnp.transpose(raw[:, pl.ds(pl.multiple_of(later, CHUNK), CHUNK), :], (1, 0, 2))

    def candidate(n, side_terms):
        slot = n + 1
        terms = candidate_terms(slot + 1, side_terms)
        rest = jnp.dot(w_rest[...], rest_taps[n * REST : (n + 3) * REST, :], preferred_element_type=F32)
        proposal = jnp.tanh(partial[slot] + terms + rest)
        old = rows_buf[here + n].astype(F32)
        new = (1.0 - update[slot]) * old + update[slot] * proposal
        rows_done[n] = jnp.where(chosen, new, old).astype(BF16)

    waiting = []
    for n in range(CHUNK):
        row_sums = sums_at(taps, n)
        carried = rows_buf[jnp.minimum(here + n + 1, ROWS - 1)]
        if n == CHUNK - 1:
            carried = jnp.where(step == STEPS - 1, inside(below[0, :STATE_CH], not_last), carried)
        if len(waiting) == LAG:
            candidate(n - LAG, waiting.pop(0))
        gates(row_sums, state_sums[n], carried, (n + 2,) if n < CHUNK - HALO else (n + 2, n + 2 - CHUNK))
        waiting.append(row_sums[2 * STATE_CH :])
        row = chunk[n]
        if n < HALO:
            noise_rim = inside(below[n, STATE_CH : STATE_CH + 16], not_last)
            row = jnp.where(step == STEPS - 1, jnp.concatenate([context_rim[HALO + n], noise_rim], axis=0), row)
            put_taps(taps, (CHUNK + n) * C3, row)
        put_taps(taps, n * C3, row)
    for n in range(CHUNK - LAG, CHUNK):
        candidate(n, waiting.pop(0))
    for n in range(1, 3):
        partial[n] = partial[CHUNK + n]
    out[...] = jnp.transpose(rows_done[...], (1, 0, 2))


def whole(*shape):
    return pl.BlockSpec(shape, lambda i: (0,) * len(shape))


def side_part(
    mine, others, noise, mine_rim, other_rim, above, below, sums, by_row, rim_sums, gate_kernel, candidate_kernel,
    active, offset,
):
    def kernel(*refs):
        side_kernel(refs[:4], refs[4:8], *refs[8:])

    smem = pl.BlockSpec(memory_space=pltpu.SMEM)
    any_space = pl.BlockSpec(memory_space=pl.ANY)
    rim_spec = whole(*mine_rim.shape)
    return pl.pallas_call(
        kernel,
        grid=(STEPS,),
        in_specs=[any_space] * 9
        + [rim_spec, rim_spec, whole(HALO, EDGE_CH, COLS), whole(HALO, EDGE_CH, COLS)]
        + [any_space] * 5
        + [smem, smem],
        out_specs=pl.BlockSpec((STATE_CH, CHUNK, COLS), lambda i: (0, i, 0)),
        out_shape=jax.ShapeDtypeStruct((STATE_CH, ROWS, COLS), BF16),
        scratch_shapes=[
            pltpu.VMEM((SIDE_CH, ROWS, COLS), BF16),
            pltpu.VMEM((3 * STATE_CH, 3 * C3), BF16),
            pltpu.VMEM((3 * STATE_CH, MAIN), BF16),
            pltpu.VMEM((STATE_CH, 3 * REST), BF16),
            pltpu.VMEM((2, CHUNK, 2 * STATE_CH, COLS), F32),
            pltpu.VMEM((ROWS, STATE_CH, COLS), BF16),
            pltpu.VMEM((HALO, 2 * STATE_CH, COLS), F32),
            pltpu.VMEM(((CHUNK + HALO) * C3, COLS), BF16),
            pltpu.VMEM((2 * HALO * C3, COLS), BF16),
            pltpu.VMEM((4 * MAIN, COLS), BF16),
            pltpu.VMEM(((CHUNK + HALO) * REST, COLS), BF16),
            pltpu.VMEM((CHUNK + HALO, STATE_CH, COLS), F32),
            pltpu.VMEM((CHUNK + HALO + 1, STATE_CH, COLS), F32),
            pltpu.VMEM((CHUNK, STATE_CH, COLS), BF16),
            pltpu.VMEM((2 * HALO, CONTEXT_CH, COLS), BF16),
            pltpu.VMEM(gate_kernel.shape, BF16),
            pltpu.VMEM(candidate_kernel.shape, BF16),
            pltpu.SemaphoreType.DMA((2, 9)),
            pltpu.SemaphoreType.DMA((2,)),
            pltpu.SemaphoreType.DMA((4,)),
        ],
        compiler_params=pltpu.CompilerParams(vmem_limit_bytes=60 * 2**20),
        cost_estimate=pl.CostEstimate(flops=17_000_000_000, bytes_accessed=20_000_000, transcendentals=0),
        name="side_part",
    )(
        *mine, *others, noise, mine_rim, other_rim, above, below, sums, by_row, rim_sums, gate_kernel, candidate_kernel,
        active, offset,
    )


def by_tap(kernel):
    return jnp.transpose(kernel, (2, 3, 0, 1)).reshape((9,) + kernel.shape[:2])


def along_x(by):
    return [(2 * x + core, 2 * ((x + by) % 4) + core) for x in range(4) for core in range(2)]


FORTH = [(2 * x + core, 2 * ((x + 1 - 2 * core) % 4) + core) for x in range(4) for core in range(2)]
BACK = [(b, a) for a, b in FORTH]
CORES = [(n, n ^ 1) for n in range(8)]


def shards(state_field, context_field, noise_latent, gate_kernel, candidate_kernel, active_tiles, tile_offset):
    owners = lax.axis_size("space")
    state = state_field[0]
    noise = noise_latent[0, 0]

    def to_core(a):
        return lax.ppermute(a, "member", CORES)

    forth = lax.ppermute(context_field, "member", FORTH)
    back = lax.ppermute(context_field, "member", BACK)
    top, low = edges(state, noise, context_field)
    above = lax.ppermute(low, "space", [(n, (n + 1) % owners) for n in range(owners)])
    below = lax.ppermute(top, "space", [((n + 1) % owners, n) for n in range(owners)])
    gate_kernel, candidate_kernel = by_tap(gate_kernel), by_tap(candidate_kernel)
    state, top = lax.optimization_barrier((state, top))
    before = state_part(0, 2, state, gate_kernel)

    before, forth, back, above, below = lax.optimization_barrier((before, forth, back, above, below))
    far = lax.ppermute(forth, "member", FORTH)
    others = [to_core(context_field), to_core(forth), to_core(back)]
    side = slice(STATE_CH + 16, STATE_CH + 16 + PIECE)
    rim = jnp.concatenate([above[:, side], below[:, side]], axis=0)
    rims = [rim] + [lax.ppermute(rim, "member", along_x(by)) for by in (3, 2, 1)]
    sums, by_row, rim_sums = state_part(2, 2, state, gate_kernel, (above, below, top), before)

    sums, rims, far = lax.optimization_barrier((sums, rims, far))
    others.append(to_core(far))
    mine_rim = jnp.stack(rims)
    mine = [context_field, forth, back, far]
    result = side_part(
        mine, others, noise, mine_rim, to_core(mine_rim), above, below, sums, by_row, rim_sums, gate_kernel,
        candidate_kernel, active_tiles.T, tile_offset.T,
    )
    return result[None]


def solution(mesh):
    return jax.shard_map(
        shards,
        mesh=mesh,
        in_specs=(
            P("member", None, "space", None),
            P("member", "space", None),
            P("member", None, None, "space", None),
            P(),
            P(),
            P(),
            P(),
        ),
        out_specs=P("member", None, "space", None),
        check_vma=False,
    )
```

```python
import functools

import jax
import jax.numpy as jnp
from jax import lax
from jax.experimental import pallas as pl
from jax.experimental.pallas import tpu as pltpu
from jax.sharding import PartitionSpec as P

STATE_CH = 96
CONTEXT_CH = 96
NOISE_CH = 8
TILE = 64
REACH = 3
HALO = 2
ROWS = 64
COLS = 256
CHUNK = 16
STEPS = ROWS // CHUNK
SIDE_CH = CONTEXT_CH + 16
PIECE = CONTEXT_CH // 8
EDGE_CH = STATE_CH + 32
RIM_CH = 16
S3 = 3 * STATE_CH
C3 = 3 * SIDE_CH
BF16 = jnp.bfloat16
F32 = jnp.float32


AHEAD = 4


def put_taps(ref, first, row):
    count = row.shape[0]
    edge = jnp.zeros((count, 1), row.dtype)
    ref[pl.ds(first, count), :] = jnp.concatenate([edge, row[:, : COLS - 1]], axis=1)
    ref[pl.ds(first + count, count), :] = row
    ref[pl.ds(first + 2 * count, count), :] = jnp.concatenate([row[:, 1:], edge], axis=1)


def logistic(x):
    return 0.5 * jnp.tanh(0.5 * x) + 0.5


def edge_kernel(state, noise, context, top, low, state_buf, noise_buf, context_buf, sems):
    copies = []
    for n, (source, buf) in enumerate(((state, state_buf), (noise, noise_buf), (context, context_buf))):
        for side, first in enumerate((0, ROWS - CHUNK)):
            rows = source.at[:, pl.ds(first, CHUNK), :]
            copies.append(pltpu.make_async_copy(rows, buf.at[side], sems.at[2 * n + side]))
    for copy in copies:
        copy.start()
    for copy in copies:
        copy.wait()
    for side, (ref, first) in enumerate(((top, 0), (low, CHUNK - HALO))):

        def rows(buf):
            return jnp.transpose(buf[side], (1, 0, 2))[first : first + HALO]

        ref[:, :STATE_CH] = rows(state_buf)
        ref[:, STATE_CH:] = jnp.zeros((HALO, EDGE_CH - STATE_CH, COLS), BF16)
        ref[:, STATE_CH : STATE_CH + NOISE_CH] = rows(noise_buf)
        ref[:, STATE_CH + 16 : STATE_CH + 16 + PIECE] = rows(context_buf)


def edges(state, noise, context):
    shape = jax.ShapeDtypeStruct((HALO, EDGE_CH, COLS), BF16)
    return pl.pallas_call(
        edge_kernel,
        in_specs=[pl.BlockSpec(memory_space=pltpu.HBM)] * 3,
        out_shape=[shape, shape],
        scratch_shapes=[pltpu.VMEM((2, count, CHUNK, COLS), BF16) for count in (STATE_CH, NOISE_CH, PIECE)]
        + [pltpu.SemaphoreType.DMA((6,))],
        compiler_params=pltpu.CompilerParams(vmem_limit_bytes=12 * 2**20),
        cost_estimate=pl.CostEstimate(flops=0, bytes_accessed=4_000_000, transcendentals=0),
        name="edges",
    )(*[pltpu.with_memory_space_constraint(a, pltpu.HBM) for a in (state, noise, context)])


def joined_taps(kernel, first, count, padded):
    parts = []
    for tap in range(9):
        parts.append(kernel[tap, :, first : first + count])
        if padded > count:
            parts.append(jnp.zeros((kernel.shape[1], padded - count), BF16))
    return jnp.concatenate(parts, axis=1)


def state_weights_kernel(gate, weights):
    weights[...] = joined_taps(gate, 0, STATE_CH, STATE_CH)


def side_weights_kernel(gate, candidate, w_side, w_reset, w_rest):
    channels = CONTEXT_CH + NOISE_CH
    w_side[: 2 * STATE_CH] = joined_taps(gate, STATE_CH, channels, SIDE_CH)
    w_side[2 * STATE_CH :] = joined_taps(candidate, STATE_CH, channels, SIDE_CH)
    for a in range(3):
        left, middle, right = (candidate[3 * a + n, :, :STATE_CH] for n in range(3))
        w_reset[a * STATE_CH : (a + 1) * STATE_CH] = jnp.concatenate(
            [left, middle, right[:, : MAIN - 2 * STATE_CH]], axis=1
        )
    w_rest[...] = jnp.concatenate([candidate[3 * a + 2, :, MAIN - 2 * STATE_CH : STATE_CH] for a in range(3)], axis=1)


def laid_out(kernel, name, shapes, *arrays):
    return pl.pallas_call(
        kernel,
        out_shape=[jax.ShapeDtypeStruct(shape, BF16) for shape in shapes],
        compiler_params=pltpu.CompilerParams(vmem_limit_bytes=12 * 2**20),
        cost_estimate=pl.CostEstimate(flops=0, bytes_accessed=3_000_000, transcendentals=0),
        name=name,
    )(*arrays)


def inside(row, is_inside):
    return jnp.where(is_inside, row, jnp.zeros_like(row))


def state_kernel(first, count, *refs):
    state, following, weights = refs[:3]
    last = first + count == STEPS
    if last:
        above, below, top = refs[3:6]
        sums, by_row, rim_sums, taps, sums_buf, sems, rim_taps = refs[8:]
    else:
        sums, by_row, taps, sums_buf, sems = refs[5 if first else 3 :]
    turn = pl.program_id(0)
    half = CHUNK // 2

    def sums_copy(part, n):
        start = pl.multiple_of((first + part) * CHUNK + n * half, half)
        source = sums_buf.at[part, pl.ds(n * half, half)]
        return pltpu.make_async_copy(source, sums.at[pl.ds(start, half)], sems.at[part, n])

    def sums_at(ref, place):
        return jnp.dot(weights[...], ref[place * S3 : (place + 3) * S3, :], preferred_element_type=F32)

    here = jnp.transpose(state[...], (1, 0, 2))
    by_row[...] = here

    @pl.when(turn == 0)
    def _():
        for n in range(AHEAD):
            put_taps(taps, n * S3, here[n])
        if last:
            not_first = lax.axis_index("space") > 0
            for n in range(HALO):
                put_taps(rim_taps, n * S3, inside(above[n, :STATE_CH], not_first))
                put_taps(rim_taps, (HALO + n) * S3, top[n, :STATE_CH])
            for n in range(HALO):
                rim_sums[n] = sums_at(rim_taps, n)

    rows = jnp.transpose(following[...], (1, 0, 2))
    for n in range(CHUNK):
        sums_buf[turn, n] = sums_at(taps, n)
        if n == half - 1:
            sums_copy(turn, 0).start()
        place = n + AHEAD
        if place < CHUNK:
            put_taps(taps, place * S3, here[place])
            continue
        row = rows[place - CHUNK]
        if place < CHUNK + HALO:
            if last:
                not_last = lax.axis_index("space") < lax.axis_size("space") - 1
                rim = inside(below[place - CHUNK, :STATE_CH], not_last)
                row = jnp.where(turn == count - 1, rim, row)
            put_taps(taps, place * S3, row)
        put_taps(taps, (place - CHUNK) * S3, row)
    sums_copy(turn, 1).start()

    @pl.when(turn == count - 1)
    def _():
        for part in range(count):
            for n in range(2):
                sums_copy(part, n).wait()


def state_part(first, count, state, weights, before=(), rims=()):
    last = first + count == STEPS
    extra = [*rims, *before]
    lead = 3 + len(rims)
    any_space = pl.BlockSpec(memory_space=pl.ANY)
    shapes = [
        pltpu.VMEM((ROWS, 2 * STATE_CH, COLS), F32),
        pltpu.VMEM((ROWS, STATE_CH, COLS), BF16),
    ]
    specs = [any_space, pl.BlockSpec((CHUNK, STATE_CH, COLS), lambda i: (first + i, 0, 0))]
    scratch = [
        pltpu.VMEM(((CHUNK + HALO) * S3, COLS), BF16),
        pltpu.VMEM((count, CHUNK, 2 * STATE_CH, COLS), F32),
        pltpu.SemaphoreType.DMA((count, 2)),
    ]
    if last:
        shapes.append(jax.ShapeDtypeStruct((HALO, 2 * STATE_CH, COLS), F32))
        specs.append(whole(HALO, 2 * STATE_CH, COLS))
        scratch.append(pltpu.VMEM((2 * HALO * S3, COLS), BF16))
    return pl.pallas_call(
        functools.partial(state_kernel, first, count),
        grid=(count,),
        in_specs=[
            pl.BlockSpec((STATE_CH, CHUNK, COLS), lambda i: (0, first + i, 0)),
            pl.BlockSpec((STATE_CH, CHUNK, COLS), lambda i: (0, jnp.minimum(first + i + 1, STEPS - 1), 0)),
            whole(*weights.shape),
        ]
        + [whole(HALO, EDGE_CH, COLS)] * len(rims)
        + [any_space] * len(before),
        out_specs=specs,
        out_shape=shapes,
        scratch_shapes=scratch,
        input_output_aliases={lead + n: n for n in range(len(before))},
        compiler_params=pltpu.CompilerParams(vmem_limit_bytes=20 * 2**20),
        cost_estimate=pl.CostEstimate(flops=3_000_000_000 * count, bytes_accessed=5_000_000 * count, transcendentals=0),
        name="state_part_%d" % first,
    )(state, state, weights, *extra)


LAG = 3
MAIN = 256
REST = S3 - MAIN


def side_kernel(
    context, forth, back, far, rims, others, other_far, noise, above, below, sums, by_row, rim_sums, w_side, w_reset, w_rest,
    active, offset, out, raw, sums_buf, rows_buf, rim_sums_buf, taps, rim_taps, reset_taps,
    rest_taps, update, partial, rows_done, rims_buf, context_rim, piece_sems, rim_sems, sums_sems, sems,
):
    step = pl.program_id(0)
    parts = ((0, CHUNK), (CHUNK, CHUNK), (2 * CHUNK, ROWS - 2 * CHUNK))
    member = lax.axis_index("member")
    x, core = member // 2, member % 2

    pieces = [(a, 0) for a in (context, forth, back, far)] + [(others, n * PIECE) for n in range(3)] + [(other_far, 0)]
    rim_pieces = [rims.at[0], far.at[PIECE], rims.at[1], rims.at[2]]
    rim_pieces += [other_far.at[PIECE + n] for n in (3, 0, 1, 2)]
    places = []
    for n in range(8):
        side = core if n < 4 else 1 - core
        near = 3 - 2 * side
        places.append(2 * lax.rem(x + (0, near, 4 - near, 2)[n % 4], 4) + side)

    def piece_copies(part):
        copies = []
        rows = pl.ds(*parts[part])
        for n, (piece, first) in enumerate(pieces):
            source = piece.at[pl.ds(first, PIECE), rows, :]
            target = raw.at[pl.ds(places[n] * PIECE, PIECE), rows, :]
            copies.append(pltpu.make_async_copy(source, target, piece_sems.at[part, n]))
        target = raw.at[pl.ds(CONTEXT_CH, NOISE_CH), rows, :]
        copies.append(pltpu.make_async_copy(noise.at[:, rows, :], target, piece_sems.at[part, 8]))
        return copies

    def sums_copy(n):
        slot = lax.rem(n, 2)
        rows = pl.ds(pl.multiple_of(n * CHUNK, CHUNK), CHUNK)
        return pltpu.make_async_copy(sums.at[rows], sums_buf.at[slot], sums_sems.at[slot])

    def sums_at(ref, place):
        return jnp.dot(w_side[...], ref[place * C3 : (place + 3) * C3, :], preferred_element_type=F32)

    not_first = lax.axis_index("space") > 0
    not_last = lax.axis_index("space") < lax.axis_size("space") - 1

    def gates(row_sums, state_sums, carried, slots):
        reset = logistic(row_sums[STATE_CH : 2 * STATE_CH] + state_sums[STATE_CH:])
        reset_row = (reset * carried.astype(F32)).astype(BF16)
        kept = logistic(row_sums[:STATE_CH] + state_sums[:STATE_CH])
        edge = jnp.zeros((STATE_CH, 1), BF16)
        right = jnp.concatenate([reset_row[:, 1:], edge], axis=1)
        first = slots[0] % 4 * MAIN
        reset_taps[first : first + STATE_CH] = jnp.concatenate([edge, reset_row[:, : COLS - 1]], axis=1)
        reset_taps[first + STATE_CH : first + 2 * STATE_CH] = reset_row
        reset_taps[first + 2 * STATE_CH : first + MAIN] = right[: MAIN - 2 * STATE_CH]
        for slot in slots:
            rest_taps[slot * REST : (slot + 1) * REST] = right[MAIN - 2 * STATE_CH :]
            update[slot] = kept

    def candidate_terms(slot, side_terms):
        first = slot % 4 * MAIN
        terms = jnp.dot(w_reset[...], reset_taps[first : first + MAIN, :], preferred_element_type=F32)
        partial[slot + 1] = terms[:STATE_CH]
        if slot > 0:
            partial[slot] += terms[STATE_CH : 2 * STATE_CH] + side_terms
        return terms[2 * STATE_CH :]

    @pl.when(step == 0)
    def _():
        raw[CONTEXT_CH + NOISE_CH :] = jnp.zeros((SIDE_CH - CONTEXT_CH - NOISE_CH, ROWS, COLS), BF16)
        first_half = piece_copies(0)
        for copy in first_half:
            copy.start()
        rest = [
            pltpu.make_async_copy(a, b, sems.at[n])
            for n, (a, b) in enumerate(((rim_sums, rim_sums_buf), (by_row, rows_buf)))
        ]
        rest += [
            pltpu.make_async_copy(piece, rims_buf.at[places[n]], rim_sems.at[n]) for n, piece in enumerate(rim_pieces)
        ]
        for copy in rest:
            copy.start()
        sums_copy(0).start()
        for part in (1, 2):
            for copy in piece_copies(part):
                copy.start()
        for copy in rest:
            copy.wait()
        for n in range(2 * HALO):
            first = n * RIM_CH
            joined = jnp.concatenate([rims_buf[m, first : first + PIECE].astype(F32) for m in range(8)], axis=0)
            context_rim[n] = inside(joined, not_first if n < HALO else not_last).astype(BF16)
        for copy in first_half:
            copy.wait()
        chunk = jnp.transpose(raw[:, :CHUNK, :], (1, 0, 2))[:AHEAD]
        for n in range(HALO):
            noise_rim = inside(above[n, STATE_CH : STATE_CH + 16], not_first)
            put_taps(rim_taps, n * C3, jnp.concatenate([context_rim[n], noise_rim], axis=0))
            put_taps(rim_taps, (HALO + n) * C3, chunk[n])
        for n in range(AHEAD):
            put_taps(taps, n * C3, chunk[n])
        for copy in piece_copies(1):
            copy.wait()
        gates(sums_at(rim_taps, 0), rim_sums_buf[0], inside(above[1, :STATE_CH], not_first), (0,))
        candidate_terms(0, None)
        row_sums = sums_at(rim_taps, 1)
        gates(row_sums, rim_sums_buf[1], rows_buf[0], (1,))
        candidate_terms(1, row_sums[2 * STATE_CH :])

    @pl.when(step == 1)
    def _():
        for copy in piece_copies(2):
            copy.wait()

    @pl.when(step + 1 < STEPS)
    def _():
        sums_copy(step + 1).start()

    sums_copy(step).wait()
    state_sums = sums_buf.at[lax.rem(step, 2)]
    here = pl.multiple_of(step * CHUNK, CHUNK)
    owner = lax.axis_index("space")
    tile = lax.broadcasted_iota(jnp.int32, (1, COLS), 1) // TILE
    chosen = jnp.zeros((1, COLS), jnp.bool_)
    for n in range(COLS // TILE):
        used = (active[n, owner] == 1) & (offset[n, owner] < REACH)
        chosen = chosen | ((tile == n) & used)
    later = pl.multiple_of(jnp.minimum(step + 1, STEPS - 1) * CHUNK, CHUNK)
    chunk = jnp.transpose(raw[:, pl.ds(here, CHUNK), :], (1, 0, 2))
    following = jnp.transpose(raw[:, pl.ds(later, CHUNK), :], (1, 0, 2))

    def candidate(n, side_terms):
        slot = n + 1
        terms = candidate_terms(slot + 1, side_terms)
        rest = jnp.dot(w_rest[...], rest_taps[n * REST : (n + 3) * REST, :], preferred_element_type=F32)
        proposal = jnp.tanh(partial[slot] + terms + rest)
        old = rows_buf[here + n].astype(F32)
        new = (1.0 - update[slot]) * old + update[slot] * proposal
        rows_done[n] = jnp.where(chosen, new, old).astype(BF16)

    waiting = []
    for n in range(CHUNK):
        row_sums = sums_at(taps, n)
        carried = rows_buf[jnp.minimum(here + n + 1, ROWS - 1)]
        if n == CHUNK - 1:
            carried = jnp.where(step == STEPS - 1, inside(below[0, :STATE_CH], not_last), carried)
        if len(waiting) == LAG:
            candidate(n - LAG, waiting.pop(0))
        gates(row_sums, state_sums[n], carried, (n + 2,) if n < CHUNK - HALO else (n + 2, n + 2 - CHUNK))
        waiting.append(row_sums[2 * STATE_CH :])
        place = n + AHEAD
        if place < CHUNK:
            put_taps(taps, place * C3, chunk[place])
            continue
        row = following[place - CHUNK]
        if place < CHUNK + HALO:
            noise_rim = inside(below[place - CHUNK, STATE_CH : STATE_CH + 16], not_last)
            rim = jnp.concatenate([context_rim[HALO + place - CHUNK], noise_rim], axis=0)
            row = jnp.where(step == STEPS - 1, rim, row)
            put_taps(taps, place * C3, row)
        put_taps(taps, (place - CHUNK) * C3, row)
    for n in range(CHUNK - LAG, CHUNK):
        candidate(n, waiting.pop(0))
    for n in range(1, 3):
        partial[n] = partial[CHUNK + n]
    out[...] = jnp.transpose(rows_done[...], (1, 0, 2))


def whole(*shape):
    return pl.BlockSpec(shape, lambda i: (0,) * len(shape))


def side_part(pieces, noise, above, below, sums, by_row, rim_sums, weights, active, offset):
    smem = pl.BlockSpec(memory_space=pltpu.SMEM)
    any_space = pl.BlockSpec(memory_space=pl.ANY)
    return pl.pallas_call(
        side_kernel,
        grid=(STEPS,),
        in_specs=[any_space] * (len(pieces) + 1)
        + [whole(HALO, EDGE_CH, COLS)] * 2
        + [any_space] * 3
        + [whole(*a.shape) for a in weights]
        + [smem, smem],
        out_specs=pl.BlockSpec((STATE_CH, CHUNK, COLS), lambda i: (0, i, 0)),
        out_shape=jax.ShapeDtypeStruct((STATE_CH, ROWS, COLS), BF16),
        scratch_shapes=[
            pltpu.VMEM((SIDE_CH, ROWS, COLS), BF16),
            pltpu.VMEM((2, CHUNK, 2 * STATE_CH, COLS), F32),
            pltpu.VMEM((ROWS, STATE_CH, COLS), BF16),
            pltpu.VMEM((HALO, 2 * STATE_CH, COLS), F32),
            pltpu.VMEM(((CHUNK + HALO) * C3, COLS), BF16),
            pltpu.VMEM((2 * HALO * C3, COLS), BF16),
            pltpu.VMEM((4 * MAIN, COLS), BF16),
            pltpu.VMEM(((CHUNK + HALO) * REST, COLS), BF16),
            pltpu.VMEM((CHUNK + HALO, STATE_CH, COLS), F32),
            pltpu.VMEM((CHUNK + HALO + 1, STATE_CH, COLS), F32),
            pltpu.VMEM((CHUNK, STATE_CH, COLS), BF16),
            pltpu.VMEM((8, 2 * HALO * RIM_CH, COLS), BF16),
            pltpu.VMEM((2 * HALO, CONTEXT_CH, COLS), BF16),
            pltpu.SemaphoreType.DMA((3, 9)),
            pltpu.SemaphoreType.DMA((8,)),
            pltpu.SemaphoreType.DMA((2,)),
            pltpu.SemaphoreType.DMA((2,)),
        ],
        compiler_params=pltpu.CompilerParams(vmem_limit_bytes=30 * 2**20),
        cost_estimate=pl.CostEstimate(flops=17_000_000_000, bytes_accessed=20_000_000, transcendentals=0),
        name="side_part",
    )(
        *pieces, noise, above, below, *[pltpu.with_memory_space_constraint(a, pltpu.VMEM) for a in (sums, by_row)],
        rim_sums, *weights, active, offset,
    )


def by_tap(kernel):
    return jnp.transpose(kernel, (2, 3, 0, 1)).reshape((9,) + kernel.shape[:2])


def along_x(by):
    return [(2 * x + core, 2 * ((x + by) % 4) + core) for x in range(4) for core in range(2)]


FORTH = [(2 * x + core, 2 * ((x + 1 - 2 * core) % 4) + core) for x in range(4) for core in range(2)]
BACK = [(b, a) for a, b in FORTH]
CORES = [(n, n ^ 1) for n in range(8)]


def shards(state_field, context_field, noise_latent, gate_kernel, candidate_kernel, active_tiles, tile_offset):
    owners = lax.axis_size("space")
    state = state_field[0]
    noise = noise_latent[0, 0]

    def to_core(a):
        return lax.ppermute(a, "member", CORES)

    forth = lax.ppermute(context_field, "member", FORTH)
    back = lax.ppermute(context_field, "member", BACK)
    top, low = edges(state, noise, context_field)
    above = lax.ppermute(low, "space", [(n, (n + 1) % owners) for n in range(owners)])
    below = lax.ppermute(top, "space", [((n + 1) % owners, n) for n in range(owners)])
    gate_kernel, candidate_kernel = by_tap(gate_kernel), by_tap(candidate_kernel)
    state, top = lax.optimization_barrier((state, top))
    (state_weights,) = laid_out(state_weights_kernel, "state_weights", [(2 * STATE_CH, 3 * S3)], gate_kernel)
    before = state_part(0, 2, state, state_weights)

    before, forth, back, above, below = lax.optimization_barrier((before, forth, back, above, below))
    side = slice(STATE_CH + 16, STATE_CH + 16 + RIM_CH)
    rim = jnp.concatenate([above[:, side], below[:, side]], axis=0).reshape(1, 2 * HALO * RIM_CH, COLS)
    far = lax.ppermute(jnp.concatenate([forth, rim], axis=0), "member", FORTH)
    rims = [rim, lax.ppermute(rim, "member", BACK), lax.ppermute(rim, "member", along_x(2))]
    others = to_core(jnp.concatenate([context_field, forth, back], axis=0))
    sums, by_row, rim_sums = state_part(2, 2, state, state_weights, before, (above, below, top))

    sums, rims, far = lax.optimization_barrier((sums, rims, far))
    rims = jnp.concatenate(rims, axis=0)
    other_far = to_core(jnp.concatenate([far, rims[1:], rims[:1]], axis=0))
    sums, gate_kernel, candidate_kernel = lax.optimization_barrier((sums, gate_kernel, candidate_kernel))
    shapes = [(3 * STATE_CH, 3 * C3), (3 * STATE_CH, MAIN), (STATE_CH, 3 * REST)]
    side_weights = laid_out(side_weights_kernel, "side_weights", shapes, gate_kernel, candidate_kernel)
    pieces = [context_field, forth, back, far, rims, others, other_far]
    result = side_part(
        pieces, noise, above, below, sums, by_row, rim_sums, side_weights, active_tiles.T, tile_offset.T
    )
    return result[None]


def solution(mesh):
    return jax.shard_map(
        shards,
        mesh=mesh,
        in_specs=(
            P("member", None, "space", None),
            P("member", "space", None),
            P("member", None, None, "space", None),
            P(),
            P(),
            P(),
            P(),
        ),
        out_specs=P("member", None, "space", None),
        check_vma=False,
    )
```

```python
import functools

import jax
import jax.numpy as jnp
from jax import lax
from jax.experimental import pallas as pl
from jax.experimental.pallas import tpu as pltpu
from jax.sharding import PartitionSpec as P

STATE_CH = 96
CONTEXT_CH = 96
NOISE_CH = 8
TILE = 64
REACH = 3
HALO = 2
ROWS = 64
COLS = 256
CHUNK = 16
STEPS = ROWS // CHUNK
SIDE_CH = CONTEXT_CH + 16
PIECE = CONTEXT_CH // 8
EDGE_CH = STATE_CH + 32
RIM_CH = 16
S3 = 3 * STATE_CH
C3 = 3 * SIDE_CH
BF16 = jnp.bfloat16
F32 = jnp.float32


AHEAD = 4


def put_taps(ref, first, row):
    count = row.shape[0]
    edge = jnp.zeros((count, 1), row.dtype)
    ref[pl.ds(first, count), :] = jnp.concatenate([edge, row[:, : COLS - 1]], axis=1)
    ref[pl.ds(first + count, count), :] = row
    ref[pl.ds(first + 2 * count, count), :] = jnp.concatenate([row[:, 1:], edge], axis=1)


def logistic_of_double(x):
    return 0.5 * jnp.tanh(x) + 0.5


def edge_kernel(state, noise, context, top, low, state_buf, noise_buf, context_buf, sems):
    copies = []
    for n, (source, buf) in enumerate(((state, state_buf), (noise, noise_buf), (context, context_buf))):
        for side, first in enumerate((0, ROWS - CHUNK)):
            rows = source.at[:, pl.ds(first, CHUNK), :]
            copies.append(pltpu.make_async_copy(rows, buf.at[side], sems.at[2 * n + side]))
    for copy in copies:
        copy.start()
    for copy in copies:
        copy.wait()
    for side, (ref, first) in enumerate(((top, 0), (low, CHUNK - HALO))):

        def rows(buf):
            return jnp.transpose(buf[side], (1, 0, 2))[first : first + HALO]

        ref[:, :STATE_CH] = rows(state_buf)
        ref[:, STATE_CH:] = jnp.zeros((HALO, EDGE_CH - STATE_CH, COLS), BF16)
        ref[:, STATE_CH : STATE_CH + NOISE_CH] = rows(noise_buf)
        ref[:, STATE_CH + 16 : STATE_CH + 16 + PIECE] = rows(context_buf)


def edges(state, noise, context):
    shape = jax.ShapeDtypeStruct((HALO, EDGE_CH, COLS), BF16)
    return pl.pallas_call(
        edge_kernel,
        in_specs=[pl.BlockSpec(memory_space=pltpu.HBM)] * 3,
        out_shape=[shape, shape],
        scratch_shapes=[pltpu.VMEM((2, count, CHUNK, COLS), BF16) for count in (STATE_CH, NOISE_CH, PIECE)]
        + [pltpu.SemaphoreType.DMA((6,))],
        compiler_params=pltpu.CompilerParams(vmem_limit_bytes=12 * 2**20),
        cost_estimate=pl.CostEstimate(flops=0, bytes_accessed=4_000_000, transcendentals=0),
        name="edges",
    )(*[pltpu.with_memory_space_constraint(a, pltpu.HBM) for a in (state, noise, context)])


def joined_taps(kernel, first, count, padded):
    parts = []
    for tap in range(9):
        parts.append(kernel[tap, :, first : first + count])
        if padded > count:
            parts.append(jnp.zeros((kernel.shape[1], padded - count), BF16))
    return jnp.concatenate(parts, axis=1)


def state_weights_kernel(gate, weights):
    weights[...] = joined_taps(gate, 0, STATE_CH, STATE_CH) * BF16(0.5)


def side_weights_kernel(gate, candidate, w_side, w_reset, w_rest):
    channels = CONTEXT_CH + NOISE_CH
    w_side[: 2 * STATE_CH] = joined_taps(gate, STATE_CH, channels, SIDE_CH) * BF16(0.5)
    w_side[2 * STATE_CH :] = joined_taps(candidate, STATE_CH, channels, SIDE_CH)
    for a in range(3):
        left, middle, right = (candidate[3 * a + n, :, :STATE_CH] for n in range(3))
        w_reset[a * STATE_CH : (a + 1) * STATE_CH] = jnp.concatenate(
            [left, middle, right[:, : MAIN - 2 * STATE_CH]], axis=1
        )
    w_rest[...] = jnp.concatenate([candidate[3 * a + 2, :, MAIN - 2 * STATE_CH : STATE_CH] for a in range(3)], axis=1)


def laid_out(kernel, name, shapes, *arrays):
    return pl.pallas_call(
        kernel,
        out_shape=[jax.ShapeDtypeStruct(shape, BF16) for shape in shapes],
        compiler_params=pltpu.CompilerParams(vmem_limit_bytes=12 * 2**20),
        cost_estimate=pl.CostEstimate(flops=0, bytes_accessed=3_000_000, transcendentals=0),
        name=name,
    )(*arrays)


def inside(row, is_inside):
    return jnp.where(is_inside, row, jnp.zeros_like(row))


def state_kernel(first, count, *refs):
    state, following, weights = refs[:3]
    last = first + count == STEPS
    if last:
        above, below, top = refs[3:6]
        sums, by_row, rim_sums, taps, rim_taps = refs[8:]
    else:
        sums, by_row, taps = refs[5 if first else 3 :]
    turn = pl.program_id(0)

    def sums_at(ref, place):
        return jnp.dot(weights[...], ref[place * S3 : (place + 3) * S3, :], preferred_element_type=F32)

    here = jnp.transpose(state[...], (1, 0, 2))
    by_row[...] = here

    @pl.when(turn == 0)
    def _():
        for n in range(AHEAD):
            put_taps(taps, n * S3, here[n])
        if last:
            not_first = lax.axis_index("space") > 0
            for n in range(HALO):
                put_taps(rim_taps, n * S3, inside(above[n, :STATE_CH], not_first))
                put_taps(rim_taps, (HALO + n) * S3, top[n, :STATE_CH])
            for n in range(HALO):
                rim_sums[n] = sums_at(rim_taps, n)

    rows = jnp.transpose(following[...], (1, 0, 2))
    for n in range(CHUNK):
        sums[n] = sums_at(taps, n)
        place = n + AHEAD
        if place < CHUNK:
            put_taps(taps, place * S3, here[place])
            continue
        row = rows[place - CHUNK]
        if place < CHUNK + HALO:
            if last:
                not_last = lax.axis_index("space") < lax.axis_size("space") - 1
                rim = inside(below[place - CHUNK, :STATE_CH], not_last)
                row = jnp.where(turn == count - 1, rim, row)
            put_taps(taps, place * S3, row)
        put_taps(taps, (place - CHUNK) * S3, row)


def state_part(first, count, state, weights, before=(), rims=()):
    last = first + count == STEPS
    extra = [*rims, *before]
    lead = 3 + len(rims)
    any_space = pl.BlockSpec(memory_space=pl.ANY)
    shapes = [
        pltpu.VMEM((ROWS, 2 * STATE_CH, COLS), F32),
        pltpu.VMEM((ROWS, STATE_CH, COLS), BF16),
    ]
    specs = [pl.BlockSpec((CHUNK, channels, COLS), lambda i: (first + i, 0, 0)) for channels in (2 * STATE_CH, STATE_CH)]
    scratch = [
        pltpu.VMEM(((CHUNK + HALO) * S3, COLS), BF16),
    ]
    if last:
        shapes.append(jax.ShapeDtypeStruct((HALO, 2 * STATE_CH, COLS), F32))
        specs.append(whole(HALO, 2 * STATE_CH, COLS))
        scratch.append(pltpu.VMEM((2 * HALO * S3, COLS), BF16))
    return pl.pallas_call(
        functools.partial(state_kernel, first, count),
        grid=(count,),
        in_specs=[
            pl.BlockSpec((STATE_CH, CHUNK, COLS), lambda i: (0, first + i, 0)),
            pl.BlockSpec((STATE_CH, CHUNK, COLS), lambda i: (0, jnp.minimum(first + i + 1, STEPS - 1), 0)),
            whole(*weights.shape),
        ]
        + [whole(HALO, EDGE_CH, COLS)] * len(rims)
        + [any_space] * len(before),
        out_specs=specs,
        out_shape=shapes,
        scratch_shapes=scratch,
        input_output_aliases={lead + n: n for n in range(len(before))},
        compiler_params=pltpu.CompilerParams(vmem_limit_bytes=20 * 2**20),
        cost_estimate=pl.CostEstimate(flops=3_000_000_000 * count, bytes_accessed=5_000_000 * count, transcendentals=0),
        name="state_part_%d" % first,
    )(state, state, weights, *extra)


LAG = 3
MAIN = 256
REST = S3 - MAIN


def side_kernel(
    context, forth, back, far, rims, others, other_far, noise, above, below, sums, by_row, rim_sums, w_side, w_reset, w_rest,
    active, offset, out, raw, taps, rim_taps, reset_taps,
    rest_taps, update, partial, rows_done, rims_buf, context_rim, piece_sems, rim_sems,
):
    step = pl.program_id(0)
    parts = ((0, CHUNK), (CHUNK, CHUNK), (2 * CHUNK, ROWS - 2 * CHUNK))
    member = lax.axis_index("member")
    x, core = member // 2, member % 2

    pieces = [(a, 0) for a in (context, forth, back, far)] + [(others, n * PIECE) for n in range(3)] + [(other_far, 0)]
    rim_pieces = [rims.at[0], far.at[PIECE], rims.at[1], rims.at[2]]
    rim_pieces += [other_far.at[PIECE + n] for n in (3, 0, 1, 2)]
    places = []
    for n in range(8):
        side = core if n < 4 else 1 - core
        near = 3 - 2 * side
        places.append(2 * lax.rem(x + (0, near, 4 - near, 2)[n % 4], 4) + side)

    def piece_copies(part):
        copies = []
        rows = pl.ds(*parts[part])
        for n, (piece, first) in enumerate(pieces):
            source = piece.at[pl.ds(first, PIECE), rows, :]
            target = raw.at[pl.ds(places[n] * PIECE, PIECE), rows, :]
            copies.append(pltpu.make_async_copy(source, target, piece_sems.at[part, n]))
        target = raw.at[pl.ds(CONTEXT_CH, NOISE_CH), rows, :]
        copies.append(pltpu.make_async_copy(noise.at[:, rows, :], target, piece_sems.at[part, 8]))
        return copies

    def sums_at(ref, place):
        return jnp.dot(w_side[...], ref[place * C3 : (place + 3) * C3, :], preferred_element_type=F32)

    not_first = lax.axis_index("space") > 0
    not_last = lax.axis_index("space") < lax.axis_size("space") - 1

    def gates(row_sums, state_sums, carried, slots):
        reset = logistic_of_double(row_sums[STATE_CH : 2 * STATE_CH] + state_sums[STATE_CH:])
        reset_row = (reset * carried.astype(F32)).astype(BF16)
        kept = logistic_of_double(row_sums[:STATE_CH] + state_sums[:STATE_CH])
        edge = jnp.zeros((STATE_CH, 1), BF16)
        right = jnp.concatenate([reset_row[:, 1:], edge], axis=1)
        first = slots[0] % 4 * MAIN
        reset_taps[first : first + STATE_CH] = jnp.concatenate([edge, reset_row[:, : COLS - 1]], axis=1)
        reset_taps[first + STATE_CH : first + 2 * STATE_CH] = reset_row
        reset_taps[first + 2 * STATE_CH : first + MAIN] = right[: MAIN - 2 * STATE_CH]
        for slot in slots:
            rest_taps[slot * REST : (slot + 1) * REST] = right[MAIN - 2 * STATE_CH :]
            update[slot] = kept

    def candidate_terms(slot, side_terms):
        first = slot % 4 * MAIN
        terms = jnp.dot(w_reset[...], reset_taps[first : first + MAIN, :], preferred_element_type=F32)
        partial[slot + 1] = terms[:STATE_CH]
        if slot > 0:
            partial[slot] += terms[STATE_CH : 2 * STATE_CH] + side_terms
        return terms[2 * STATE_CH :]

    @pl.when(step == 0)
    def _():
        raw[CONTEXT_CH + NOISE_CH :] = jnp.zeros((SIDE_CH - CONTEXT_CH - NOISE_CH, ROWS, COLS), BF16)
        first_half = piece_copies(0)
        for copy in first_half:
            copy.start()
        rest = [
            pltpu.make_async_copy(piece, rims_buf.at[places[n]], rim_sems.at[n]) for n, piece in enumerate(rim_pieces)
        ]
        for copy in rest:
            copy.start()
        for part in (1, 2):
            for copy in piece_copies(part):
                copy.start()
        for copy in rest:
            copy.wait()
        for n in range(2 * HALO):
            first = n * RIM_CH
            joined = jnp.concatenate([rims_buf[m, first : first + PIECE].astype(F32) for m in range(8)], axis=0)
            context_rim[n] = inside(joined, not_first if n < HALO else not_last).astype(BF16)
        for copy in first_half:
            copy.wait()
        chunk = jnp.transpose(raw[:, :CHUNK, :], (1, 0, 2))[:AHEAD]
        for n in range(HALO):
            noise_rim = inside(above[n, STATE_CH : STATE_CH + 16], not_first)
            put_taps(rim_taps, n * C3, jnp.concatenate([context_rim[n], noise_rim], axis=0))
            put_taps(rim_taps, (HALO + n) * C3, chunk[n])
        for n in range(AHEAD):
            put_taps(taps, n * C3, chunk[n])
        for copy in piece_copies(1):
            copy.wait()
        gates(sums_at(rim_taps, 0), rim_sums[0], inside(above[1, :STATE_CH], not_first), (0,))
        candidate_terms(0, None)
        row_sums = sums_at(rim_taps, 1)
        gates(row_sums, rim_sums[1], by_row[0], (1,))
        candidate_terms(1, row_sums[2 * STATE_CH :])

    @pl.when(step == 1)
    def _():
        for copy in piece_copies(2):
            copy.wait()

    here = pl.multiple_of(step * CHUNK, CHUNK)
    owner = lax.axis_index("space")
    tile = lax.broadcasted_iota(jnp.int32, (1, COLS), 1) // TILE
    chosen = jnp.zeros((1, COLS), jnp.bool_)
    for n in range(COLS // TILE):
        used = (active[n, owner] == 1) & (offset[n, owner] < REACH)
        chosen = chosen | ((tile == n) & used)
    later = pl.multiple_of(jnp.minimum(step + 1, STEPS - 1) * CHUNK, CHUNK)
    chunk = jnp.transpose(raw[:, pl.ds(here, CHUNK), :], (1, 0, 2))
    following = jnp.transpose(raw[:, pl.ds(later, CHUNK), :], (1, 0, 2))

    def candidate(n, side_terms):
        slot = n + 1
        terms = candidate_terms(slot + 1, side_terms)
        rest = jnp.dot(w_rest[...], rest_taps[n * REST : (n + 3) * REST, :], preferred_element_type=F32)
        proposal = jnp.tanh(partial[slot] + terms + rest)
        old = by_row[here + n].astype(F32)
        new = (1.0 - update[slot]) * old + update[slot] * proposal
        rows_done[n] = jnp.where(chosen, new, old).astype(BF16)

    waiting = []
    for n in range(CHUNK):
        row_sums = sums_at(taps, n)
        carried = by_row[jnp.minimum(here + n + 1, ROWS - 1)]
        if n == CHUNK - 1:
            carried = jnp.where(step == STEPS - 1, inside(below[0, :STATE_CH], not_last), carried)
        if len(waiting) == LAG:
            candidate(n - LAG, waiting.pop(0))
        gates(row_sums, sums[n], carried, (n + 2,) if n < CHUNK - HALO else (n + 2, n + 2 - CHUNK))
        waiting.append(row_sums[2 * STATE_CH :])
        place = n + AHEAD
        if place < CHUNK:
            put_taps(taps, place * C3, chunk[place])
            continue
        row = following[place - CHUNK]
        if place < CHUNK + HALO:
            noise_rim = inside(below[place - CHUNK, STATE_CH : STATE_CH + 16], not_last)
            rim = jnp.concatenate([context_rim[HALO + place - CHUNK], noise_rim], axis=0)
            row = jnp.where(step == STEPS - 1, rim, row)
            put_taps(taps, place * C3, row)
        put_taps(taps, (place - CHUNK) * C3, row)
    for n in range(CHUNK - LAG, CHUNK):
        candidate(n, waiting.pop(0))
    for n in range(1, 3):
        partial[n] = partial[CHUNK + n]
    out[...] = jnp.transpose(rows_done[...], (1, 0, 2))


def whole(*shape):
    return pl.BlockSpec(shape, lambda i: (0,) * len(shape))


def side_part(pieces, noise, above, below, sums, by_row, rim_sums, weights, active, offset):
    smem = pl.BlockSpec(memory_space=pltpu.SMEM)
    any_space = pl.BlockSpec(memory_space=pl.ANY)
    return pl.pallas_call(
        side_kernel,
        grid=(STEPS,),
        in_specs=[any_space] * (len(pieces) + 1)
        + [whole(HALO, EDGE_CH, COLS)] * 2
        + [pl.BlockSpec((CHUNK, 2 * STATE_CH, COLS), lambda i: (i, 0, 0))]
        + [whole(*a.shape) for a in (by_row, rim_sums, *weights)]
        + [smem, smem],
        out_specs=pl.BlockSpec((STATE_CH, CHUNK, COLS), lambda i: (0, i, 0)),
        out_shape=jax.ShapeDtypeStruct((STATE_CH, ROWS, COLS), BF16),
        scratch_shapes=[
            pltpu.VMEM((SIDE_CH, ROWS, COLS), BF16),
            pltpu.VMEM(((CHUNK + HALO) * C3, COLS), BF16),
            pltpu.VMEM((2 * HALO * C3, COLS), BF16),
            pltpu.VMEM((4 * MAIN, COLS), BF16),
            pltpu.VMEM(((CHUNK + HALO) * REST, COLS), BF16),
            pltpu.VMEM((CHUNK + HALO, STATE_CH, COLS), F32),
            pltpu.VMEM((CHUNK + HALO + 1, STATE_CH, COLS), F32),
            pltpu.VMEM((CHUNK, STATE_CH, COLS), BF16),
            pltpu.VMEM((8, 2 * HALO * RIM_CH, COLS), BF16),
            pltpu.VMEM((2 * HALO, CONTEXT_CH, COLS), BF16),
            pltpu.SemaphoreType.DMA((3, 9)),
            pltpu.SemaphoreType.DMA((8,)),
        ],
        compiler_params=pltpu.CompilerParams(vmem_limit_bytes=24 * 2**20),
        cost_estimate=pl.CostEstimate(flops=17_000_000_000, bytes_accessed=20_000_000, transcendentals=0),
        name="side_part",
    )(
        *pieces, noise, above, below, *[pltpu.with_memory_space_constraint(a, pltpu.VMEM) for a in (sums, by_row)],
        rim_sums, *weights, active, offset,
    )


def by_tap(kernel):
    return jnp.transpose(kernel, (2, 3, 0, 1)).reshape((9,) + kernel.shape[:2])


def along_x(by):
    return [(2 * x + core, 2 * ((x + by) % 4) + core) for x in range(4) for core in range(2)]


FORTH = [(2 * x + core, 2 * ((x + 1 - 2 * core) % 4) + core) for x in range(4) for core in range(2)]
BACK = [(b, a) for a, b in FORTH]
CORES = [(n, n ^ 1) for n in range(8)]


def shards(state_field, context_field, noise_latent, gate_kernel, candidate_kernel, active_tiles, tile_offset):
    owners = lax.axis_size("space")
    state = state_field[0]
    noise = noise_latent[0, 0]

    def to_core(a):
        return lax.ppermute(a, "member", CORES)

    forth = lax.ppermute(context_field, "member", FORTH)
    back = lax.ppermute(context_field, "member", BACK)
    top, low = edges(state, noise, context_field)
    above = lax.ppermute(low, "space", [(n, (n + 1) % owners) for n in range(owners)])
    below = lax.ppermute(top, "space", [((n + 1) % owners, n) for n in range(owners)])
    gate_kernel, candidate_kernel = by_tap(gate_kernel), by_tap(candidate_kernel)
    state, top = lax.optimization_barrier((state, top))
    (state_weights,) = laid_out(state_weights_kernel, "state_weights", [(2 * STATE_CH, 3 * S3)], gate_kernel)
    before = state_part(0, 2, state, state_weights)

    before, forth, back, above, below = lax.optimization_barrier((before, forth, back, above, below))
    side = slice(STATE_CH + 16, STATE_CH + 16 + RIM_CH)
    rim = jnp.concatenate([above[:, side], below[:, side]], axis=0).reshape(1, 2 * HALO * RIM_CH, COLS)
    far = lax.ppermute(jnp.concatenate([forth, rim], axis=0), "member", FORTH)
    rims = [rim, lax.ppermute(rim, "member", BACK), lax.ppermute(rim, "member", along_x(2))]
    others = to_core(jnp.concatenate([context_field, forth, back], axis=0))
    sums, by_row, rim_sums = state_part(2, 2, state, state_weights, before, (above, below, top))

    sums, rims, far = lax.optimization_barrier((sums, rims, far))
    rims = jnp.concatenate(rims, axis=0)
    other_far = to_core(jnp.concatenate([far, rims[1:], rims[:1]], axis=0))
    sums, gate_kernel, candidate_kernel = lax.optimization_barrier((sums, gate_kernel, candidate_kernel))
    shapes = [(3 * STATE_CH, 3 * C3), (3 * STATE_CH, MAIN), (STATE_CH, 3 * REST)]
    side_weights = laid_out(side_weights_kernel, "side_weights", shapes, gate_kernel, candidate_kernel)
    pieces = [context_field, forth, back, far, rims, others, other_far]
    result = side_part(
        pieces, noise, above, below, sums, by_row, rim_sums, side_weights, active_tiles.T, tile_offset.T
    )
    return result[None]


def solution(mesh):
    return jax.shard_map(
        shards,
        mesh=mesh,
        in_specs=(
            P("member", None, "space", None),
            P("member", "space", None),
            P("member", None, None, "space", None),
            P(),
            P(),
            P(),
            P(),
        ),
        out_specs=P("member", None, "space", None),
        check_vma=False,
    )
```

```python
import functools

import jax
import jax.numpy as jnp
from jax import lax
from jax.experimental import pallas as pl
from jax.experimental.pallas import tpu as pltpu
from jax.sharding import PartitionSpec as P

STATE_CH = 96
CONTEXT_CH = 96
NOISE_CH = 8
TILE = 64
REACH = 3
HALO = 2
ROWS = 64
COLS = 256
CHUNK = 16
STEPS = ROWS // CHUNK
SIDE_CH = CONTEXT_CH + 16
PIECE = CONTEXT_CH // 8
EDGE_CH = STATE_CH + 32
RIM_CH = 16
S3 = 3 * STATE_CH
C3 = 3 * SIDE_CH
BF16 = jnp.bfloat16
F32 = jnp.float32


AHEAD = 4


def put_taps(ref, first, row):
    count = row.shape[0]
    edge = jnp.zeros((count, 1), row.dtype)
    ref[pl.ds(first, count), :] = jnp.concatenate([edge, row[:, : COLS - 1]], axis=1)
    ref[pl.ds(first + count, count), :] = row
    ref[pl.ds(first + 2 * count, count), :] = jnp.concatenate([row[:, 1:], edge], axis=1)


def logistic_of_double(x):
    return 0.5 * jnp.tanh(x) + 0.5


def edge_kernel(state, noise, context, top, low, state_buf, noise_buf, context_buf, sems):
    copies = []
    for n, (source, buf) in enumerate(((state, state_buf), (noise, noise_buf), (context, context_buf))):
        for side, first in enumerate((0, ROWS - CHUNK)):
            rows = source.at[:, pl.ds(first, CHUNK), :]
            copies.append(pltpu.make_async_copy(rows, buf.at[side], sems.at[2 * n + side]))
    for copy in copies:
        copy.start()
    for copy in copies:
        copy.wait()
    for side, (ref, first) in enumerate(((top, 0), (low, CHUNK - HALO))):

        def rows(buf):
            return jnp.transpose(buf[side], (1, 0, 2))[first : first + HALO]

        ref[:, :STATE_CH] = rows(state_buf)
        ref[:, STATE_CH:] = jnp.zeros((HALO, EDGE_CH - STATE_CH, COLS), BF16)
        ref[:, STATE_CH : STATE_CH + NOISE_CH] = rows(noise_buf)
        ref[:, STATE_CH + 16 : STATE_CH + 16 + PIECE] = rows(context_buf)


def edges(state, noise, context):
    shape = jax.ShapeDtypeStruct((HALO, EDGE_CH, COLS), BF16)
    return pl.pallas_call(
        edge_kernel,
        in_specs=[pl.BlockSpec(memory_space=pltpu.HBM)] * 3,
        out_shape=[shape, shape],
        scratch_shapes=[pltpu.VMEM((2, count, CHUNK, COLS), BF16) for count in (STATE_CH, NOISE_CH, PIECE)]
        + [pltpu.SemaphoreType.DMA((6,))],
        compiler_params=pltpu.CompilerParams(vmem_limit_bytes=12 * 2**20),
        cost_estimate=pl.CostEstimate(flops=0, bytes_accessed=4_000_000, transcendentals=0),
        name="edges",
    )(*[pltpu.with_memory_space_constraint(a, pltpu.HBM) for a in (state, noise, context)])


def joined_taps(kernel, first, count, padded):
    parts = []
    for tap in range(9):
        parts.append(kernel[tap, :, first : first + count])
        if padded > count:
            parts.append(jnp.zeros((kernel.shape[1], padded - count), BF16))
    return jnp.concatenate(parts, axis=1)


def state_weights_kernel(gate, weights):
    weights[...] = joined_taps(gate, 0, STATE_CH, STATE_CH) * BF16(0.5)


def side_weights_kernel(gate, candidate, w_side, w_reset, w_rest):
    channels = CONTEXT_CH + NOISE_CH
    w_side[: 2 * STATE_CH] = joined_taps(gate, STATE_CH, channels, SIDE_CH) * BF16(0.5)
    w_side[2 * STATE_CH :] = joined_taps(candidate, STATE_CH, channels, SIDE_CH)
    for a in range(3):
        left, middle, right = (candidate[3 * a + n, :, :STATE_CH] for n in range(3))
        w_reset[a * STATE_CH : (a + 1) * STATE_CH] = jnp.concatenate(
            [left, middle, right[:, : MAIN - 2 * STATE_CH]], axis=1
        )
    w_rest[...] = jnp.concatenate([candidate[3 * a + 2, :, MAIN - 2 * STATE_CH : STATE_CH] for a in range(3)], axis=1)


def laid_out(kernel, name, shapes, *arrays):
    return pl.pallas_call(
        kernel,
        out_shape=[jax.ShapeDtypeStruct(shape, BF16) for shape in shapes],
        compiler_params=pltpu.CompilerParams(vmem_limit_bytes=12 * 2**20),
        cost_estimate=pl.CostEstimate(flops=0, bytes_accessed=3_000_000, transcendentals=0),
        name=name,
    )(*arrays)


def inside(row, is_inside):
    return jnp.where(is_inside, row, jnp.zeros_like(row))


def state_kernel(first, count, *refs):
    state, following, weights = refs[:3]
    last = first + count == STEPS
    if last:
        above, below, top = refs[3:6]
        sums, by_row, rim_sums, taps, rim_taps = refs[8:]
    else:
        sums, by_row, taps = refs[5 if first else 3 :]
    turn = pl.program_id(0)

    def sums_at(ref, place):
        return jnp.dot(weights[...], ref[place * S3 : (place + 3) * S3, :], preferred_element_type=F32)

    here = jnp.transpose(state[...], (1, 0, 2))
    by_row[...] = here

    @pl.when(turn == 0)
    def _():
        for n in range(AHEAD):
            put_taps(taps, n * S3, here[n])
        if last:
            not_first = lax.axis_index("space") > 0
            for n in range(HALO):
                put_taps(rim_taps, n * S3, inside(above[n, :STATE_CH], not_first))
                put_taps(rim_taps, (HALO + n) * S3, top[n, :STATE_CH])
            for n in range(HALO):
                rim_sums[n] = sums_at(rim_taps, n)

    rows = jnp.transpose(following[...], (1, 0, 2))
    for n in range(CHUNK):
        sums[n] = sums_at(taps, n)
        place = n + AHEAD
        if place < CHUNK:
            put_taps(taps, place * S3, here[place])
            continue
        row = rows[place - CHUNK]
        if place < CHUNK + HALO:
            if last:
                not_last = lax.axis_index("space") < lax.axis_size("space") - 1
                rim = inside(below[place - CHUNK, :STATE_CH], not_last)
                row = jnp.where(turn == count - 1, rim, row)
            put_taps(taps, place * S3, row)
        put_taps(taps, (place - CHUNK) * S3, row)


def state_part(first, count, state, weights, before=(), rims=()):
    last = first + count == STEPS
    extra = [*rims, *before]
    lead = 3 + len(rims)
    any_space = pl.BlockSpec(memory_space=pl.ANY)
    shapes = [
        pltpu.VMEM((ROWS, 2 * STATE_CH, COLS), F32),
        pltpu.VMEM((ROWS, STATE_CH, COLS), BF16),
    ]
    specs = [pl.BlockSpec((CHUNK, channels, COLS), lambda i: (first + i, 0, 0)) for channels in (2 * STATE_CH, STATE_CH)]
    scratch = [
        pltpu.VMEM(((CHUNK + HALO) * S3, COLS), BF16),
    ]
    if last:
        shapes.append(jax.ShapeDtypeStruct((HALO, 2 * STATE_CH, COLS), F32))
        specs.append(whole(HALO, 2 * STATE_CH, COLS))
        scratch.append(pltpu.VMEM((2 * HALO * S3, COLS), BF16))
    return pl.pallas_call(
        functools.partial(state_kernel, first, count),
        grid=(count,),
        in_specs=[
            pl.BlockSpec((STATE_CH, CHUNK, COLS), lambda i: (0, first + i, 0)),
            pl.BlockSpec((STATE_CH, CHUNK, COLS), lambda i: (0, jnp.minimum(first + i + 1, STEPS - 1), 0)),
            whole(*weights.shape),
        ]
        + [whole(HALO, EDGE_CH, COLS)] * len(rims)
        + [any_space] * len(before),
        out_specs=specs,
        out_shape=shapes,
        scratch_shapes=scratch,
        input_output_aliases={lead + n: n for n in range(len(before))},
        compiler_params=pltpu.CompilerParams(vmem_limit_bytes=20 * 2**20),
        cost_estimate=pl.CostEstimate(flops=3_000_000_000 * count, bytes_accessed=5_000_000 * count, transcendentals=0),
        name="state_part_%d" % first,
    )(state, state, weights, *extra)


LAG = 3
MAIN = 256
REST = S3 - MAIN


def side_kernel(
    context, forth, back, far, rims, others, other_far, noise, above, below, sums, by_row, rim_sums, w_side, w_reset, w_rest,
    active, offset, out, raw, taps, rim_taps, reset_taps,
    rest_taps, update, partial, rows_done, rims_buf, context_rim, piece_sems, rim_sems,
):
    step = pl.program_id(0)
    parts = ((0, CHUNK), (CHUNK, CHUNK), (2 * CHUNK, ROWS - 2 * CHUNK))
    member = lax.axis_index("member")
    x, core = member // 2, member % 2

    pieces = [(a, 0) for a in (context, forth, back, far)] + [(others, n * PIECE) for n in range(3)] + [(other_far, 0)]
    rim_pieces = [rims.at[0], far.at[PIECE], rims.at[1], rims.at[2]]
    rim_pieces += [other_far.at[PIECE + n] for n in (3, 0, 1, 2)]
    places = []
    for n in range(8):
        side = core if n < 4 else 1 - core
        near = 3 - 2 * side
        places.append(2 * lax.rem(x + (0, near, 4 - near, 2)[n % 4], 4) + side)

    def piece_copies(part):
        copies = []
        rows = pl.ds(*parts[part])
        for n, (piece, first) in enumerate(pieces):
            source = piece.at[pl.ds(first, PIECE), rows, :]
            target = raw.at[pl.ds(places[n] * PIECE, PIECE), rows, :]
            copies.append(pltpu.make_async_copy(source, target, piece_sems.at[part, n]))
        target = raw.at[pl.ds(CONTEXT_CH, NOISE_CH), rows, :]
        copies.append(pltpu.make_async_copy(noise.at[:, rows, :], target, piece_sems.at[part, 8]))
        return copies

    def sums_at(ref, place):
        return jnp.dot(w_side[...], ref[place * C3 : (place + 3) * C3, :], preferred_element_type=F32)

    not_first = lax.axis_index("space") > 0
    not_last = lax.axis_index("space") < lax.axis_size("space") - 1

    def gates(row_sums, state_sums, carried, slots):
        reset = logistic_of_double(row_sums[STATE_CH : 2 * STATE_CH] + state_sums[STATE_CH:])
        reset_row = (reset * carried.astype(F32)).astype(BF16)
        kept = logistic_of_double(row_sums[:STATE_CH] + state_sums[:STATE_CH])
        edge = jnp.zeros((STATE_CH, 1), BF16)
        right = jnp.concatenate([reset_row[:, 1:], edge], axis=1)
        first = slots[0] % 4 * MAIN
        reset_taps[first : first + STATE_CH] = jnp.concatenate([edge, reset_row[:, : COLS - 1]], axis=1)
        reset_taps[first + STATE_CH : first + 2 * STATE_CH] = reset_row
        reset_taps[first + 2 * STATE_CH : first + MAIN] = right[: MAIN - 2 * STATE_CH]
        for slot in slots:
            rest_taps[slot * REST : (slot + 1) * REST] = right[MAIN - 2 * STATE_CH :]
            update[slot] = kept

    def candidate_terms(slot, side_terms):
        first = slot % 4 * MAIN
        terms = jnp.dot(w_reset[...], reset_taps[first : first + MAIN, :], preferred_element_type=F32)
        partial[slot + 1] = terms[:STATE_CH]
        if slot > 0:
            partial[slot] += terms[STATE_CH : 2 * STATE_CH] + side_terms
        return terms[2 * STATE_CH :]

    @pl.when(step == 0)
    def _():
        raw[CONTEXT_CH + NOISE_CH :] = jnp.zeros((SIDE_CH - CONTEXT_CH - NOISE_CH, ROWS, COLS), BF16)
        first_half = piece_copies(0)
        for copy in first_half:
            copy.start()
        rest = [
            pltpu.make_async_copy(piece, rims_buf.at[places[n]], rim_sems.at[n]) for n, piece in enumerate(rim_pieces)
        ]
        for copy in rest:
            copy.start()
        for part in (1, 2):
            for copy in piece_copies(part):
                copy.start()
        for copy in rest:
            copy.wait()
        for n in range(2 * HALO):
            first = n * RIM_CH
            joined = jnp.concatenate([rims_buf[m, first : first + PIECE].astype(F32) for m in range(8)], axis=0)
            context_rim[n] = inside(joined, not_first if n < HALO else not_last).astype(BF16)
        for copy in first_half:
            copy.wait()
        chunk = jnp.transpose(raw[:, :CHUNK, :], (1, 0, 2))[:AHEAD]
        for n in range(HALO):
            noise_rim = inside(above[n, STATE_CH : STATE_CH + 16], not_first)
            put_taps(rim_taps, n * C3, jnp.concatenate([context_rim[n], noise_rim], axis=0))
            put_taps(rim_taps, (HALO + n) * C3, chunk[n])
        for n in range(AHEAD):
            put_taps(taps, n * C3, chunk[n])
        for copy in piece_copies(1):
            copy.wait()
        gates(sums_at(rim_taps, 0), rim_sums[0], inside(above[1, :STATE_CH], not_first), (0,))
        candidate_terms(0, None)
        row_sums = sums_at(rim_taps, 1)
        gates(row_sums, rim_sums[1], by_row[0], (1,))
        candidate_terms(1, row_sums[2 * STATE_CH :])

    @pl.when(step == 1)
    def _():
        for copy in piece_copies(2):
            copy.wait()

    here = pl.multiple_of(step * CHUNK, CHUNK)
    owner = lax.axis_index("space")
    tile = lax.broadcasted_iota(jnp.int32, (1, COLS), 1) // TILE
    chosen = jnp.zeros((1, COLS), jnp.bool_)
    for n in range(COLS // TILE):
        used = (active[n, owner] == 1) & (offset[n, owner] < REACH)
        chosen = chosen | ((tile == n) & used)
    later = pl.multiple_of(jnp.minimum(step + 1, STEPS - 1) * CHUNK, CHUNK)
    chunk = jnp.transpose(raw[:, pl.ds(here, CHUNK), :], (1, 0, 2))
    following = jnp.transpose(raw[:, pl.ds(later, CHUNK), :], (1, 0, 2))

    def candidate(n, side_terms):
        slot = n + 1
        terms = candidate_terms(slot + 1, side_terms)
        rest = jnp.dot(w_rest[...], rest_taps[n * REST : (n + 3) * REST, :], preferred_element_type=F32)
        proposal = jnp.tanh(partial[slot] + terms + rest)
        old = by_row[here + n].astype(F32)
        new = (1.0 - update[slot]) * old + update[slot] * proposal
        rows_done[n] = jnp.where(chosen, new, old).astype(BF16)

    waiting = []
    for n in range(CHUNK):
        row_sums = sums_at(taps, n)
        carried = by_row[jnp.minimum(here + n + 1, ROWS - 1)]
        if n == CHUNK - 1:
            carried = jnp.where(step == STEPS - 1, inside(below[0, :STATE_CH], not_last), carried)
        if len(waiting) == LAG:
            candidate(n - LAG, waiting.pop(0))
        gates(row_sums, sums[n], carried, (n + 2,) if n < CHUNK - HALO else (n + 2, n + 2 - CHUNK))
        waiting.append(row_sums[2 * STATE_CH :])
        place = n + AHEAD
        if place < CHUNK:
            put_taps(taps, place * C3, chunk[place])
            continue
        row = following[place - CHUNK]
        if place < CHUNK + HALO:
            noise_rim = inside(below[place - CHUNK, STATE_CH : STATE_CH + 16], not_last)
            rim = jnp.concatenate([context_rim[HALO + place - CHUNK], noise_rim], axis=0)
            row = jnp.where(step == STEPS - 1, rim, row)
            put_taps(taps, place * C3, row)
        put_taps(taps, (place - CHUNK) * C3, row)
    for n in range(CHUNK - LAG, CHUNK):
        candidate(n, waiting.pop(0))
    for n in range(1, 3):
        partial[n] = partial[CHUNK + n]
    out[...] = jnp.transpose(rows_done[...], (1, 0, 2))


def whole(*shape):
    return pl.BlockSpec(shape, lambda i: (0,) * len(shape))


def side_part(pieces, noise, above, below, sums, by_row, rim_sums, weights, active, offset):
    smem = pl.BlockSpec(memory_space=pltpu.SMEM)
    any_space = pl.BlockSpec(memory_space=pl.ANY)
    return pl.pallas_call(
        side_kernel,
        grid=(STEPS,),
        in_specs=[any_space] * (len(pieces) + 1)
        + [whole(HALO, EDGE_CH, COLS)] * 2
        + [pl.BlockSpec((CHUNK, 2 * STATE_CH, COLS), lambda i: (i, 0, 0))]
        + [whole(*a.shape) for a in (by_row, rim_sums, *weights)]
        + [smem, smem],
        out_specs=pl.BlockSpec((STATE_CH, CHUNK, COLS), lambda i: (0, i, 0)),
        out_shape=jax.ShapeDtypeStruct((STATE_CH, ROWS, COLS), BF16),
        scratch_shapes=[
            pltpu.VMEM((SIDE_CH, ROWS, COLS), BF16),
            pltpu.VMEM(((CHUNK + HALO) * C3, COLS), BF16),
            pltpu.VMEM((2 * HALO * C3, COLS), BF16),
            pltpu.VMEM((4 * MAIN, COLS), BF16),
            pltpu.VMEM(((CHUNK + HALO) * REST, COLS), BF16),
            pltpu.VMEM((CHUNK + HALO, STATE_CH, COLS), F32),
            pltpu.VMEM((CHUNK + HALO + 1, STATE_CH, COLS), F32),
            pltpu.VMEM((CHUNK, STATE_CH, COLS), BF16),
            pltpu.VMEM((8, 2 * HALO * RIM_CH, COLS), BF16),
            pltpu.VMEM((2 * HALO, CONTEXT_CH, COLS), BF16),
            pltpu.SemaphoreType.DMA((3, 9)),
            pltpu.SemaphoreType.DMA((8,)),
        ],
        compiler_params=pltpu.CompilerParams(vmem_limit_bytes=24 * 2**20),
        cost_estimate=pl.CostEstimate(flops=17_000_000_000, bytes_accessed=20_000_000, transcendentals=0),
        name="side_part",
    )(
        *pieces, noise, above, below, *[pltpu.with_memory_space_constraint(a, pltpu.VMEM) for a in (sums, by_row)],
        rim_sums, *weights, active, offset,
    )


def by_tap(kernel):
    return jnp.transpose(kernel, (2, 3, 0, 1)).reshape((9,) + kernel.shape[:2])


def along_x(by):
    return [(2 * x + core, 2 * ((x + by) % 4) + core) for x in range(4) for core in range(2)]


FORTH = [(2 * x + core, 2 * ((x + 1 - 2 * core) % 4) + core) for x in range(4) for core in range(2)]
BACK = [(b, a) for a, b in FORTH]
CORES = [(n, n ^ 1) for n in range(8)]


def shards(state_field, context_field, noise_latent, gate_kernel, candidate_kernel, active_tiles, tile_offset):
    owners = lax.axis_size("space")
    state = state_field[0]
    noise = noise_latent[0, 0]

    def to_core(a):
        return lax.ppermute(a, "member", CORES)

    forth = lax.ppermute(context_field, "member", FORTH)
    back = lax.ppermute(context_field, "member", BACK)
    top, low = edges(state, noise, context_field)
    above = lax.ppermute(low, "space", [(n, (n + 1) % owners) for n in range(owners)])
    below = lax.ppermute(top, "space", [((n + 1) % owners, n) for n in range(owners)])
    gate_kernel, candidate_kernel = by_tap(gate_kernel), by_tap(candidate_kernel)
    state, top = lax.optimization_barrier((state, top))
    (state_weights,) = laid_out(state_weights_kernel, "state_weights", [(2 * STATE_CH, 3 * S3)], gate_kernel)
    before = state_part(0, 2, state, state_weights)

    before, forth, back, above, below = lax.optimization_barrier((before, forth, back, above, below))
    side = slice(STATE_CH + 16, STATE_CH + 16 + RIM_CH)
    rim = jnp.concatenate([above[:, side], below[:, side]], axis=0).reshape(1, 2 * HALO * RIM_CH, COLS)
    far = lax.ppermute(jnp.concatenate([forth, rim], axis=0), "member", FORTH)
    others = to_core(jnp.concatenate([context_field, forth, back], axis=0))
    before = state_part(2, 1, state, state_weights, before)

    before, rim = lax.optimization_barrier((before, rim))
    rims = [rim, lax.ppermute(rim, "member", BACK), lax.ppermute(rim, "member", along_x(2))]
    sums, by_row, rim_sums = state_part(3, 1, state, state_weights, before, (above, below, top))

    sums, rims, far = lax.optimization_barrier((sums, rims, far))
    rims = jnp.concatenate(rims, axis=0)
    other_far = to_core(jnp.concatenate([far, rims[1:], rims[:1]], axis=0))
    sums, gate_kernel, candidate_kernel = lax.optimization_barrier((sums, gate_kernel, candidate_kernel))
    shapes = [(3 * STATE_CH, 3 * C3), (3 * STATE_CH, MAIN), (STATE_CH, 3 * REST)]
    side_weights = laid_out(side_weights_kernel, "side_weights", shapes, gate_kernel, candidate_kernel)
    pieces = [context_field, forth, back, far, rims, others, other_far]
    result = side_part(
        pieces, noise, above, below, sums, by_row, rim_sums, side_weights, active_tiles.T, tile_offset.T
    )
    return result[None]


def solution(mesh):
    return jax.shard_map(
        shards,
        mesh=mesh,
        in_specs=(
            P("member", None, "space", None),
            P("member", "space", None),
            P("member", None, None, "space", None),
            P(),
            P(),
            P(),
            P(),
        ),
        out_specs=P("member", None, "space", None),
        check_vma=False,
    )
```

```python
import functools

import jax
import jax.numpy as jnp
from jax import lax
from jax.experimental import pallas as pl
from jax.experimental.pallas import tpu as pltpu
from jax.sharding import PartitionSpec as P

STATE_CH = 96
CONTEXT_CH = 96
NOISE_CH = 8
TILE = 64
REACH = 3
HALO = 2
ROWS = 64
COLS = 256
CHUNK = 16
STEPS = ROWS // CHUNK
SIDE_CH = CONTEXT_CH + 16
PIECE = CONTEXT_CH // 8
EDGE_CH = STATE_CH + 32
RIM_CH = 16
S3 = 3 * STATE_CH
C3 = 3 * SIDE_CH
BF16 = jnp.bfloat16
F32 = jnp.float32


AHEAD = 4


def put_taps(ref, first, row):
    count = row.shape[0]
    edge = jnp.zeros((count, 1), row.dtype)
    ref[pl.ds(first, count), :] = jnp.concatenate([edge, row[:, : COLS - 1]], axis=1)
    ref[pl.ds(first + count, count), :] = row
    ref[pl.ds(first + 2 * count, count), :] = jnp.concatenate([row[:, 1:], edge], axis=1)


def logistic_of_double(x):
    return 0.5 * jnp.tanh(x) + 0.5


def edge_kernel(state, noise, context, top, low, state_buf, noise_buf, context_buf, sems):
    copies = []
    for n, (source, buf) in enumerate(((state, state_buf), (noise, noise_buf), (context, context_buf))):
        for side, first in enumerate((0, ROWS - CHUNK)):
            rows = source.at[:, pl.ds(first, CHUNK), :]
            copies.append(pltpu.make_async_copy(rows, buf.at[side], sems.at[2 * n + side]))
    for copy in copies:
        copy.start()
    for copy in copies:
        copy.wait()
    for side, (ref, first) in enumerate(((top, 0), (low, CHUNK - HALO))):

        def rows(buf):
            return jnp.transpose(buf[side], (1, 0, 2))[first : first + HALO]

        ref[:, :STATE_CH] = rows(state_buf)
        ref[:, STATE_CH:] = jnp.zeros((HALO, EDGE_CH - STATE_CH, COLS), BF16)
        ref[:, STATE_CH : STATE_CH + NOISE_CH] = rows(noise_buf)
        ref[:, STATE_CH + 16 : STATE_CH + 16 + PIECE] = rows(context_buf)


def edges(state, noise, context):
    shape = jax.ShapeDtypeStruct((HALO, EDGE_CH, COLS), BF16)
    return pl.pallas_call(
        edge_kernel,
        in_specs=[pl.BlockSpec(memory_space=pltpu.HBM)] * 3,
        out_shape=[shape, shape],
        scratch_shapes=[pltpu.VMEM((2, count, CHUNK, COLS), BF16) for count in (STATE_CH, NOISE_CH, PIECE)]
        + [pltpu.SemaphoreType.DMA((6,))],
        compiler_params=pltpu.CompilerParams(vmem_limit_bytes=12 * 2**20),
        cost_estimate=pl.CostEstimate(flops=0, bytes_accessed=4_000_000, transcendentals=0),
        name="edges",
    )(*[pltpu.with_memory_space_constraint(a, pltpu.HBM) for a in (state, noise, context)])


def joined_taps(kernel, first, count, padded):
    parts = []
    for tap in range(9):
        parts.append(kernel[tap, :, first : first + count])
        if padded > count:
            parts.append(jnp.zeros((kernel.shape[1], padded - count), BF16))
    return jnp.concatenate(parts, axis=1)


def state_weights_kernel(gate, weights):
    weights[...] = joined_taps(gate, 0, STATE_CH, STATE_CH) * BF16(0.5)


def side_weights_kernel(gate, candidate, w_side, w_reset, w_rest):
    channels = CONTEXT_CH + NOISE_CH
    w_side[: 2 * STATE_CH] = joined_taps(gate, STATE_CH, channels, SIDE_CH) * BF16(0.5)
    w_side[2 * STATE_CH :] = joined_taps(candidate, STATE_CH, channels, SIDE_CH)
    for a in range(3):
        left, middle, right = (candidate[3 * a + n, :, :STATE_CH] for n in range(3))
        w_reset[a * STATE_CH : (a + 1) * STATE_CH] = jnp.concatenate(
            [left, middle, right[:, : MAIN - 2 * STATE_CH]], axis=1
        )
    w_rest[...] = jnp.concatenate([candidate[3 * a + 2, :, MAIN - 2 * STATE_CH : STATE_CH] for a in range(3)], axis=1)


def laid_out(kernel, name, shapes, *arrays):
    return pl.pallas_call(
        kernel,
        out_shape=[jax.ShapeDtypeStruct(shape, BF16) for shape in shapes],
        compiler_params=pltpu.CompilerParams(vmem_limit_bytes=12 * 2**20),
        cost_estimate=pl.CostEstimate(flops=0, bytes_accessed=3_000_000, transcendentals=0),
        name=name,
    )(*arrays)


def inside(row, is_inside):
    return jnp.where(is_inside, row, jnp.zeros_like(row))


def state_kernel(first, count, *refs):
    state, following, weights = refs[:3]
    last = first + count == STEPS
    if last:
        above, below, top = refs[3:6]
        sums, by_row, rim_sums, taps, rim_taps = refs[8:]
    else:
        sums, by_row, taps = refs[5 if first else 3 :]
    turn = pl.program_id(0)

    def sums_at(ref, place):
        return jnp.dot(weights[...], ref[place * S3 : (place + 3) * S3, :], preferred_element_type=F32)

    here = jnp.transpose(state[...], (1, 0, 2))
    by_row[...] = here

    @pl.when(turn == 0)
    def _():
        for n in range(AHEAD):
            put_taps(taps, n * S3, here[n])
        if last:
            not_first = lax.axis_index("space") > 0
            for n in range(HALO):
                put_taps(rim_taps, n * S3, inside(above[n, :STATE_CH], not_first))
                put_taps(rim_taps, (HALO + n) * S3, top[n, :STATE_CH])
            for n in range(HALO):
                rim_sums[n] = sums_at(rim_taps, n)

    rows = jnp.transpose(following[...], (1, 0, 2))
    for n in range(CHUNK):
        sums[n] = sums_at(taps, n)
        place = n + AHEAD
        if place < CHUNK:
            put_taps(taps, place * S3, here[place])
            continue
        row = rows[place - CHUNK]
        if place < CHUNK + HALO:
            if last:
                not_last = lax.axis_index("space") < lax.axis_size("space") - 1
                rim = inside(below[place - CHUNK, :STATE_CH], not_last)
                row = jnp.where(turn == count - 1, rim, row)
            put_taps(taps, place * S3, row)
        put_taps(taps, (place - CHUNK) * S3, row)


def state_part(first, count, state, weights, before=(), rims=()):
    last = first + count == STEPS
    extra = [*rims, *before]
    lead = 3 + len(rims)
    any_space = pl.BlockSpec(memory_space=pl.ANY)
    shapes = [
        pltpu.VMEM((ROWS, 2 * STATE_CH, COLS), F32),
        pltpu.VMEM((ROWS, STATE_CH, COLS), BF16),
    ]
    specs = [pl.BlockSpec((CHUNK, channels, COLS), lambda i: (first + i, 0, 0)) for channels in (2 * STATE_CH, STATE_CH)]
    scratch = [
        pltpu.VMEM(((CHUNK + HALO) * S3, COLS), BF16),
    ]
    if last:
        shapes.append(jax.ShapeDtypeStruct((HALO, 2 * STATE_CH, COLS), F32))
        specs.append(whole(HALO, 2 * STATE_CH, COLS))
        scratch.append(pltpu.VMEM((2 * HALO * S3, COLS), BF16))
    return pl.pallas_call(
        functools.partial(state_kernel, first, count),
        grid=(count,),
        in_specs=[
            pl.BlockSpec((STATE_CH, CHUNK, COLS), lambda i: (0, first + i, 0)),
            pl.BlockSpec((STATE_CH, CHUNK, COLS), lambda i: (0, jnp.minimum(first + i + 1, STEPS - 1), 0)),
            whole(*weights.shape),
        ]
        + [whole(HALO, EDGE_CH, COLS)] * len(rims)
        + [any_space] * len(before),
        out_specs=specs,
        out_shape=shapes,
        scratch_shapes=scratch,
        input_output_aliases={lead + n: n for n in range(len(before))},
        compiler_params=pltpu.CompilerParams(vmem_limit_bytes=20 * 2**20),
        cost_estimate=pl.CostEstimate(flops=3_000_000_000 * count, bytes_accessed=5_000_000 * count, transcendentals=0),
        name="state_part_%d" % first,
    )(state, state, weights, *extra)


LAG = 3
MAIN = 256
REST = S3 - MAIN


def side_kernel(
    context, forth, back, far, rims, others, other_far, noise, above, below, sums, by_row, rim_sums, w_side, w_reset, w_rest,
    active, offset, out, raw, taps, rim_taps, reset_taps,
    rest_taps, update, partial, rows_done, rims_buf, context_rim, chunk, piece_sems, rim_sems,
):
    step = pl.program_id(0)
    parts = ((0, CHUNK), (CHUNK, CHUNK), (2 * CHUNK, ROWS - 2 * CHUNK))
    member = lax.axis_index("member")
    x, core = member // 2, member % 2

    pieces = [(a, 0) for a in (context, forth, back, far)] + [(others, n * PIECE) for n in range(3)] + [(other_far, 0)]
    rim_pieces = [rims.at[0], far.at[PIECE], rims.at[1], rims.at[2]]
    rim_pieces += [other_far.at[PIECE + n] for n in (3, 0, 1, 2)]
    places = []
    for n in range(8):
        side = core if n < 4 else 1 - core
        near = 3 - 2 * side
        places.append(2 * lax.rem(x + (0, near, 4 - near, 2)[n % 4], 4) + side)

    def piece_copies(part):
        copies = []
        rows = pl.ds(*parts[part])
        for n, (piece, first) in enumerate(pieces):
            source = piece.at[pl.ds(first, PIECE), rows, :]
            target = raw.at[pl.ds(places[n] * PIECE, PIECE), rows, :]
            copies.append(pltpu.make_async_copy(source, target, piece_sems.at[part, n]))
        target = raw.at[pl.ds(CONTEXT_CH, NOISE_CH), rows, :]
        copies.append(pltpu.make_async_copy(noise.at[:, rows, :], target, piece_sems.at[part, 8]))
        return copies

    def sums_at(ref, place):
        return jnp.dot(w_side[...], ref[place * C3 : (place + 3) * C3, :], preferred_element_type=F32)

    not_first = lax.axis_index("space") > 0
    not_last = lax.axis_index("space") < lax.axis_size("space") - 1

    def gates(row_sums, state_sums, carried, slots):
        reset = logistic_of_double(row_sums[STATE_CH : 2 * STATE_CH] + state_sums[STATE_CH:])
        reset_row = (reset * carried.astype(F32)).astype(BF16)
        kept = logistic_of_double(row_sums[:STATE_CH] + state_sums[:STATE_CH])
        edge = jnp.zeros((STATE_CH, 1), BF16)
        right = jnp.concatenate([reset_row[:, 1:], edge], axis=1)
        first = slots[0] % 4 * MAIN
        reset_taps[first : first + STATE_CH] = jnp.concatenate([edge, reset_row[:, : COLS - 1]], axis=1)
        reset_taps[first + STATE_CH : first + 2 * STATE_CH] = reset_row
        reset_taps[first + 2 * STATE_CH : first + MAIN] = right[: MAIN - 2 * STATE_CH]
        for slot in slots:
            rest_taps[slot * REST : (slot + 1) * REST] = right[MAIN - 2 * STATE_CH :]
            update[slot] = kept

    def candidate_terms(slot, side_terms):
        first = slot % 4 * MAIN
        terms = jnp.dot(w_reset[...], reset_taps[first : first + MAIN, :], preferred_element_type=F32)
        partial[slot + 1] = terms[:STATE_CH]
        if slot > 0:
            partial[slot] += terms[STATE_CH : 2 * STATE_CH] + side_terms
        return terms[2 * STATE_CH :]

    @pl.when(step == 0)
    def _():
        raw[CONTEXT_CH + NOISE_CH :] = jnp.zeros((SIDE_CH - CONTEXT_CH - NOISE_CH, ROWS, COLS), BF16)
        first_half = piece_copies(0)
        for copy in first_half:
            copy.start()
        rest = [
            pltpu.make_async_copy(piece, rims_buf.at[places[n]], rim_sems.at[n]) for n, piece in enumerate(rim_pieces)
        ]
        for copy in rest:
            copy.start()
        for part in (1, 2):
            for copy in piece_copies(part):
                copy.start()
        for copy in rest:
            copy.wait()
        for n in range(2 * HALO):
            first = n * RIM_CH
            joined = jnp.concatenate([rims_buf[m, first : first + PIECE].astype(F32) for m in range(8)], axis=0)
            context_rim[n] = inside(joined, not_first if n < HALO else not_last).astype(BF16)
        for copy in first_half:
            copy.wait()
        chunk[...] = jnp.transpose(raw[:, :CHUNK, :], (1, 0, 2))
        for n in range(HALO):
            noise_rim = inside(above[n, STATE_CH : STATE_CH + 16], not_first)
            put_taps(rim_taps, n * C3, jnp.concatenate([context_rim[n], noise_rim], axis=0))
            put_taps(rim_taps, (HALO + n) * C3, chunk[n])
        for n in range(AHEAD):
            put_taps(taps, n * C3, chunk[n])
        for copy in piece_copies(1):
            copy.wait()
        gates(sums_at(rim_taps, 0), rim_sums[0], inside(above[1, :STATE_CH], not_first), (0,))
        candidate_terms(0, None)
        row_sums = sums_at(rim_taps, 1)
        gates(row_sums, rim_sums[1], by_row[0], (1,))
        candidate_terms(1, row_sums[2 * STATE_CH :])

    @pl.when(step == 1)
    def _():
        for copy in piece_copies(2):
            copy.wait()

    here = pl.multiple_of(step * CHUNK, CHUNK)
    owner = lax.axis_index("space")
    tile = lax.broadcasted_iota(jnp.int32, (1, COLS), 1) // TILE
    chosen = jnp.zeros((1, COLS), jnp.bool_)
    for n in range(COLS // TILE):
        used = (active[n, owner] == 1) & (offset[n, owner] < REACH)
        chosen = chosen | ((tile == n) & used)
    later = pl.multiple_of(jnp.minimum(step + 1, STEPS - 1) * CHUNK, CHUNK)

    def candidate(n, side_terms):
        slot = n + 1
        terms = candidate_terms(slot + 1, side_terms)
        rest = jnp.dot(w_rest[...], rest_taps[n * REST : (n + 3) * REST, :], preferred_element_type=F32)
        proposal = jnp.tanh(partial[slot] + terms + rest)
        old = by_row[here + n].astype(F32)
        new = (1.0 - update[slot]) * old + update[slot] * proposal
        rows_done[n] = jnp.where(chosen, new, old).astype(BF16)

    waiting = []
    for n in range(CHUNK):
        row_sums = sums_at(taps, n)
        carried = by_row[jnp.minimum(here + n + 1, ROWS - 1)]
        if n == CHUNK - 1:
            carried = jnp.where(step == STEPS - 1, inside(below[0, :STATE_CH], not_last), carried)
        if len(waiting) == LAG:
            candidate(n - LAG, waiting.pop(0))
        gates(row_sums, sums[n], carried, (n + 2,) if n < CHUNK - HALO else (n + 2, n + 2 - CHUNK))
        waiting.append(row_sums[2 * STATE_CH :])
        place = n + AHEAD
        if place < CHUNK:
            put_taps(taps, place * C3, chunk[place])
            continue
        if place == CHUNK:
            following = jnp.transpose(raw[:, pl.ds(later, CHUNK), :], (1, 0, 2))
            chunk[...] = following
        row = following[place - CHUNK]
        if place < CHUNK + HALO:
            noise_rim = inside(below[place - CHUNK, STATE_CH : STATE_CH + 16], not_last)
            rim = jnp.concatenate([context_rim[HALO + place - CHUNK], noise_rim], axis=0)
            row = jnp.where(step == STEPS - 1, rim, row)
            put_taps(taps, place * C3, row)
        put_taps(taps, (place - CHUNK) * C3, row)
    for n in range(CHUNK - LAG, CHUNK):
        candidate(n, waiting.pop(0))
    for n in range(1, 3):
        partial[n] = partial[CHUNK + n]
    out[...] = jnp.transpose(rows_done[...], (1, 0, 2))


def whole(*shape):
    return pl.BlockSpec(shape, lambda i: (0,) * len(shape))


def side_part(pieces, noise, above, below, sums, by_row, rim_sums, weights, active, offset):
    smem = pl.BlockSpec(memory_space=pltpu.SMEM)
    any_space = pl.BlockSpec(memory_space=pl.ANY)
    return pl.pallas_call(
        side_kernel,
        grid=(STEPS,),
        in_specs=[any_space] * (len(pieces) + 1)
        + [whole(HALO, EDGE_CH, COLS)] * 2
        + [pl.BlockSpec((CHUNK, 2 * STATE_CH, COLS), lambda i: (i, 0, 0))]
        + [whole(*a.shape) for a in (by_row, rim_sums, *weights)]
        + [smem, smem],
        out_specs=pl.BlockSpec((STATE_CH, CHUNK, COLS), lambda i: (0, i, 0)),
        out_shape=jax.ShapeDtypeStruct((STATE_CH, ROWS, COLS), BF16),
        scratch_shapes=[
            pltpu.VMEM((SIDE_CH, ROWS, COLS), BF16),
            pltpu.VMEM(((CHUNK + HALO) * C3, COLS), BF16),
            pltpu.VMEM((2 * HALO * C3, COLS), BF16),
            pltpu.VMEM((4 * MAIN, COLS), BF16),
            pltpu.VMEM(((CHUNK + HALO) * REST, COLS), BF16),
            pltpu.VMEM((CHUNK + HALO, STATE_CH, COLS), F32),
            pltpu.VMEM((CHUNK + HALO + 1, STATE_CH, COLS), F32),
            pltpu.VMEM((CHUNK, STATE_CH, COLS), BF16),
            pltpu.VMEM((8, 2 * HALO * RIM_CH, COLS), BF16),
            pltpu.VMEM((2 * HALO, CONTEXT_CH, COLS), BF16),
            pltpu.VMEM((CHUNK, SIDE_CH, COLS), BF16),
            pltpu.SemaphoreType.DMA((3, 9)),
            pltpu.SemaphoreType.DMA((8,)),
        ],
        compiler_params=pltpu.CompilerParams(vmem_limit_bytes=24 * 2**20),
        cost_estimate=pl.CostEstimate(flops=17_000_000_000, bytes_accessed=20_000_000, transcendentals=0),
        name="side_part",
    )(
        *pieces, noise, above, below, *[pltpu.with_memory_space_constraint(a, pltpu.VMEM) for a in (sums, by_row)],
        rim_sums, *weights, active, offset,
    )


def by_tap(kernel):
    return jnp.transpose(kernel, (2, 3, 0, 1)).reshape((9,) + kernel.shape[:2])


def along_x(by):
    return [(2 * x + core, 2 * ((x + by) % 4) + core) for x in range(4) for core in range(2)]


FORTH = [(2 * x + core, 2 * ((x + 1 - 2 * core) % 4) + core) for x in range(4) for core in range(2)]
BACK = [(b, a) for a, b in FORTH]
CORES = [(n, n ^ 1) for n in range(8)]


def shards(state_field, context_field, noise_latent, gate_kernel, candidate_kernel, active_tiles, tile_offset):
    owners = lax.axis_size("space")
    state = state_field[0]
    noise = noise_latent[0, 0]

    def to_core(a):
        return lax.ppermute(a, "member", CORES)

    forth = lax.ppermute(context_field, "member", FORTH)
    back = lax.ppermute(context_field, "member", BACK)
    top, low = edges(state, noise, context_field)
    above = lax.ppermute(low, "space", [(n, (n + 1) % owners) for n in range(owners)])
    below = lax.ppermute(top, "space", [((n + 1) % owners, n) for n in range(owners)])
    gate_kernel, candidate_kernel = by_tap(gate_kernel), by_tap(candidate_kernel)
    gate_kernel, top = lax.optimization_barrier((gate_kernel, top))
    (state_weights,) = laid_out(state_weights_kernel, "state_weights", [(2 * STATE_CH, 3 * S3)], gate_kernel)
    before = state_part(0, 2, state, state_weights)

    before, forth, back, above, below = lax.optimization_barrier((before, forth, back, above, below))
    side = slice(STATE_CH + 16, STATE_CH + 16 + RIM_CH)
    rim = jnp.concatenate([above[:, side], below[:, side]], axis=0).reshape(1, 2 * HALO * RIM_CH, COLS)
    far = lax.ppermute(jnp.concatenate([forth, rim], axis=0), "member", FORTH)
    others = to_core(jnp.concatenate([context_field, forth, back], axis=0))
    before = state_part(2, 1, state, state_weights, before)

    before, rim = lax.optimization_barrier((before, rim))
    rims = [rim, lax.ppermute(rim, "member", BACK), lax.ppermute(rim, "member", along_x(2))]
    sums, by_row, rim_sums = state_part(3, 1, state, state_weights, before, (above, below, top))

    sums, rims, far = lax.optimization_barrier((sums, rims, far))
    rims = jnp.concatenate(rims, axis=0)
    other_far = to_core(jnp.concatenate([far, rims[1:], rims[:1]], axis=0))
    sums, gate_kernel, candidate_kernel = lax.optimization_barrier((sums, gate_kernel, candidate_kernel))
    shapes = [(3 * STATE_CH, 3 * C3), (3 * STATE_CH, MAIN), (STATE_CH, 3 * REST)]
    side_weights = laid_out(side_weights_kernel, "side_weights", shapes, gate_kernel, candidate_kernel)
    pieces = [context_field, forth, back, far, rims, others, other_far]
    result = side_part(
        pieces, noise, above, below, sums, by_row, rim_sums, side_weights, active_tiles.T, tile_offset.T
    )
    return result[None]


def solution(mesh):
    return jax.shard_map(
        shards,
        mesh=mesh,
        in_specs=(
            P("member", None, "space", None),
            P("member", "space", None),
            P("member", None, None, "space", None),
            P(),
            P(),
            P(),
            P(),
        ),
        out_specs=P("member", None, "space", None),
        check_vma=False,
    )
```
